32 devices in a mesh: rep: 4 (over y, x), exp: 8 (over z, core).
Axes of the slice: x: 2, y: 2, z: 4, core: 2. Of those that a mesh axis runs over, the one named last changes fastest.
Arguments:
- tokens: bfloat16 [1024, 3584], P(('rep', 'exp')), parts along dimension 0, may hold values from -6 to 6
- expert_ids: int32 [1024, 8], P(('rep', 'exp')), parts along dimension 0, may hold values from 0 to 383, all different within a row; in each aligned block of 32 rows (0 to 31, 32 to 63, ...) at most 2 rows name the same one
- gate_scores: float32 [1024, 8], P(('rep', 'exp')), parts along dimension 0, may hold values from 0.02 to 0.4
- gate_weight: bfloat16 [3584, 16384], P(None, 'exp'), may hold values from -0.09375 to 0.09375
- up_weight: bfloat16 [3584, 16384], P(None, 'exp'), may hold values from -0.09375 to 0.09375
- down_weight: bfloat16 [16384, 3584], P('exp'), may hold values from -0.125 to 0.125
Outputs:
- combined: bfloat16 [1024, 3584], P(('rep', 'exp')), parts along dimension 0
- expert_load: float32 [1536], P('rep'), parts along dimension 0
The draws below stay inside these ranges and needn't reach their ends.
There are 4 independent parts, one for each index of `rep`. The reference program is written for one: setup_inputs(seed, part) draws one part's arguments, and reference() takes and returns one part's arrays. A program takes and returns all parts, laid end to end along the dimension named above; an argument that names none is the same for every part. Nothing has to cross between parts.
Inputs may be any that keep to these rules, and one draw needn't show every extreme that they name: `expert_ids`: each row names 8 different experts. Among the rows of one device no expert is named by more than 2 rows, a bound that some block reaches.
All inputs are finite; a program needn't handle non-finite values.
Results may differ from the reference program's by a relative error of at most 0.0057.
Values may be sent and summed in bfloat16 or wider, within the bound.
A program may use at most 128 MiB of HBM per device.

```python
import math
import jax
import jax.numpy as jnp
import numpy as np

D = 3584
FF = 2048
EXPERTS_ALL = 384
TOP = 8
EXPERTS = 8
TOK_DEV = 32
CAP = 2
HID_DEV = 2048
TOKENS = 256
N_EXP = 8


def levels(rng, shape, cuts, low, largest):
    gain = 1.0
    for position, parts in cuts:
        heights = jax.random.uniform(jax.random.fold_in(jax.random.fold_in(rng, 6), position), (parts,), jnp.float32, low / len(cuts), largest / len(cuts))
        gain = gain * jnp.repeat(jnp.exp(heights), shape[position] // parts).reshape((-1,) + (1,) * (len(shape) - 1 - position))
    return gain


def assign_block(stream_key, own, number, rows, amount, top, reach, slope):
    ranking = jax.random.permutation(stream_key, amount)
    crowded, common = portions_of(amount, rows * top, reach, slope, True), portions_of(amount, rows * top, reach, slope, False)
    places = jnp.arange(amount)

    def named(tallies, rotation):
        used = int((tallies > 0).sum())
        fixed = max(1, used // 4)
        shifted = fixed + (places - fixed + rotation * (used - fixed)) % max(1, amount - fixed)
        return jnp.zeros((amount,), jnp.int32).at[ranking[jnp.where(places < fixed, places, shifted)]].set(jnp.asarray(tallies, jnp.int32))

    tallies = jnp.where(number % 4 == 0, named(crowded, number // 4), named(common, number - number // 4 - 1))
    mixed = jax.random.permutation(jax.random.fold_in(own, 3), amount)
    giver, receiver = mixed[0:amount // 2 * 2:2], mixed[1:amount // 2 * 2:2]
    slack = jnp.minimum(tallies[giver] - 1, reach - tallies[receiver]) // 2
    slack = jnp.where((giver == ranking[0]) | (receiver == ranking[0]) | (tallies[receiver] == 0), 0, jnp.maximum(slack, 0))
    shifted = jax.random.randint(jax.random.fold_in(own, 4), (amount // 2,), 0, 1 << 20) % (slack + 1)
    tallies = tallies.at[giver].add(-shifted).at[receiver].add(shifted)
    labels = jnp.searchsorted(jnp.cumsum(tallies), jnp.arange(rows * top), side="right").astype(jnp.int32)
    grid = labels.reshape(top, rows).T
    grid = grid[jax.random.permutation(jax.random.fold_in(own, 1), rows)]
    rotation = jax.random.randint(jax.random.fold_in(own, 2), (rows, 1), 0, top)
    return jnp.take_along_axis(grid, (jnp.arange(top)[None, :] + rotation) % top, axis=1)


def portions_of(amount, total, limit, slope, full):
    loads = [(1 << 20) // math.isqrt(standing ** slope) + 1 for standing in range(1, amount + 1)]
    largest = limit if full else min(limit, max(-(-total // amount), total * loads[0] // sum(loads)))
    least = 1 if total - largest >= amount - 1 else 0
    holding, rest = [largest] + [least] * (amount - 1), total - largest - least * (amount - 1)
    while rest > 0:
        movable = [i for i in range(1, amount) if holding[i] < largest] or [i for i in range(1, amount) if holding[i] < limit]
        mass, budget = sum([loads[i] for i in movable]), rest
        for i in movable:
            addition = min(limit - holding[i], max(1, budget * loads[i] // mass), rest)
            holding[i] = holding[i] + addition
            rest = rest - addition
    return np.array(holding)


def noise(own_key, dims, deviation, limit, split=(), kind=jnp.bfloat16):
    values = jax.random.normal(own_key, dims, jnp.float32) * deviation
    if len(split) > 0:
        values = levels(own_key, dims, split, -0.22, 0.18) * values
    return jnp.clip(values, min=-limit, max=limit).astype(kind)


def setup_inputs(seed: int = 0, part: int = 0) -> dict:
    seeds = jax.random.split(jax.random.key(seed), 7)
    own_keys = jax.random.split(jax.random.fold_in(seeds[6], part), 7)
    tokens = noise(own_keys[0], (TOKENS, D), 1.0, 6.0, ((0, 8),))
    expert_ids_keys = jax.random.split(jax.random.fold_in(own_keys[1], 1), TOKENS // TOK_DEV)
    expert_ids_turns = jax.random.permutation(jax.random.fold_in(own_keys[1], 3), TOKENS // TOK_DEV)
    expert_ids = jax.vmap(lambda own, number: assign_block(jax.random.fold_in(own_keys[1], 2), own, number, TOK_DEV, EXPERTS_ALL, TOP, CAP, 1))(expert_ids_keys, expert_ids_turns).reshape((TOKENS, TOP))
    gate_scores = jnp.clip(jnp.exp(math.log(0.4) - 2.9957323 * jax.random.uniform(own_keys[2], (TOKENS, TOP), jnp.float32) ** levels(own_keys[2], (TOKENS, TOP), ((0, 8),), -0.2, 0.2)), 0.02, 0.4)
    gate_weight = noise(seeds[3], (D, EXPERTS * FF), D ** -0.5, 0.09375, ((1, 8),))
    up_weight = noise(seeds[4], (D, EXPERTS * FF), D ** -0.5, 0.09375, ((1, 8),))
    down_weight = noise(seeds[5], (EXPERTS * FF, D), FF ** -0.5, 0.125, ((0, 8),))
    return {"tokens": tokens, "expert_ids": expert_ids, "gate_scores": gate_scores, "gate_weight": gate_weight, "up_weight": up_weight, "down_weight": down_weight}


def reference(tokens, expert_ids, gate_scores, gate_weight, up_weight, down_weight):
    expert_load = jax.ops.segment_sum(gate_scores.reshape(-1), expert_ids.reshape(-1).astype(jnp.int32), num_segments=EXPERTS_ALL)
    rows_bound = N_EXP * CAP
    combined_sum = jnp.zeros((TOKENS, D), jnp.float32)
    for expert in range(EXPERTS):
        matches = expert_ids == expert
        row_gate = jnp.sum(jnp.where(matches, gate_scores, 0.0), axis=1)
        named = jnp.any(matches, axis=1)
        chosen = jnp.nonzero(named, size=rows_bound, fill_value=0)[0].astype(jnp.int32)
        is_live = jnp.arange(rows_bound, dtype=jnp.int32) < jnp.sum(named.astype(jnp.int32))
        picked = tokens[chosen]
        first = expert * FF
        gate_act = jnp.dot(picked, gate_weight[:, first:first + FF], preferred_element_type=jnp.float32)
        up_act = jnp.dot(picked, up_weight[:, first:first + FF], preferred_element_type=jnp.float32)
        hidden = (jax.nn.silu(gate_act) * up_act).astype(jnp.bfloat16)
        result = jnp.zeros((rows_bound, D), jnp.float32)
        for block_index in range(FF // HID_DEV):
            low = block_index * HID_DEV
            partial_value = jnp.dot(hidden[:, low:low + HID_DEV], down_weight[first + low:first + low + HID_DEV, :], preferred_element_type=jnp.float32).astype(jnp.bfloat16)
            result = result + partial_value.astype(jnp.float32)
        row_scale = jnp.where(is_live, row_gate[chosen], 0.0)
        combined_sum = combined_sum.at[chosen].add(row_scale[:, None] * result)
    return combined_sum.astype(jnp.bfloat16), expert_load
```

```python
import functools

import jax
import jax.numpy as jnp
from jax import lax
from jax.experimental import pallas as pl
from jax.experimental.pallas import tpu as pltpu
from jax.sharding import PartitionSpec as P

FF = 2048
EXPERTS_ALL = 384
CAP = 2
SLAB = 16
GROUP = 8
MESH = pl.DeviceIdType.MESH
BF16 = jnp.bfloat16
F32 = jnp.float32


def dot(a, b):
    return jnp.dot(a, b, preferred_element_type=F32)


def iota(shape, dim):
    return lax.broadcasted_iota(jnp.int32, shape, dim)


def one_hot(mask):
    return jnp.where(mask, 1.0, 0.0).astype(BF16)


def slab_place(i, segs):
    dev, seg, row = i // SLAB, (i % SLAB) // CAP, i % CAP
    return jnp.where(seg < segs, seg * (GROUP * CAP) + dev * CAP + row, -1)


def kernel(
    cfg,
    tokens_hbm, ids_hbm, scores_hbm, gate_hbm, up_hbm, down_hbm,
    out_ref, load_ref,
    tokens_v, ids_v, scores_v, gate_v, up_v, down_v,
    send_v, arrived_v, x_v, back_v, returned_v, mass_v, mixing_v, hidden_v,
    small_sem, gate_sem, up_sem, down_sem,
    send_sem, recv_sem, mass_send_sem, mass_recv_sem, back_send_sem, back_recv_sem,
):
    n, spread, segs, seg_w, pieces, piece_w, k_parts, k_rows = cfg
    groups = n // GROUP
    tok_rows, top = ids_v.shape
    lanes = mixing_lanes(n)
    me = lax.axis_index("exp")
    back_w = piece_w // segs

    small = [
        pltpu.make_async_copy(ids_hbm, ids_v, small_sem.at[0]),
        pltpu.make_async_copy(scores_hbm, scores_v, small_sem.at[1]),
        pltpu.make_async_copy(tokens_hbm, tokens_v, small_sem.at[2]),
    ]
    for copy in small:
        copy.start()

    def gate_copy(s):
        return pltpu.make_async_copy(
            gate_hbm.at[pl.ds(s * seg_w, seg_w), :], gate_v.at[s], gate_sem.at[s]
        )

    def up_copy(s):
        return pltpu.make_async_copy(
            up_hbm.at[pl.ds(s * seg_w, seg_w), :], up_v.at[s], up_sem.at[s]
        )

    def down_copy(p, k):
        return pltpu.make_async_copy(
            down_hbm.at[pl.ds(k * k_rows, k_rows), pl.ds(p * piece_w, piece_w)],
            down_v.at[p * k_parts + k],
            down_sem.at[p * k_parts + k],
        )

    for s in range(segs):
        gate_copy(s).start()
        up_copy(s).start()
    for p in range(pieces):
        for k in range(k_parts):
            down_copy(p, k).start()

    def others(body):
        def step(i, carry):
            body(lax.rem(me + i, n))
            return carry

        lax.fori_loop(1, n, step, 0, unroll=n <= 16)

    barrier = pltpu.get_barrier_semaphore()
    others(lambda d: pl.semaphore_signal(barrier, inc=1, device_id={"exp": d}, device_id_type=MESH))

    for copy in small[:2]:
        copy.wait()
    ids = ids_v[...]
    scores = scores_v[...]
    all_ids = iota((tok_rows, EXPERTS_ALL), 1)
    slot = iota((tok_rows, lanes), 1)
    slot_expert = jnp.where(slot < n * CAP, slot // (CAP * spread), -1)
    mass = jnp.zeros((tok_rows, EXPERTS_ALL), F32)
    gates = jnp.zeros((tok_rows, lanes), F32)
    hits = jnp.zeros((tok_rows, lanes), F32)
    for k in range(top):
        id_k, score_k = ids[:, k : k + 1], scores[:, k : k + 1]
        mass = mass + jnp.where(id_k == all_ids, score_k, 0.0)
        found = id_k == slot_expert
        gates = gates + jnp.where(found, score_k, 0.0)
        hits = hits + jnp.where(found, 1.0, 0.0)
    earlier = one_hot(iota((tok_rows, tok_rows), 1) < iota((tok_rows, tok_rows), 0))
    position = dot(earlier, hits.astype(BF16))
    placed = (hits > 0.5) & (position == (slot % CAP).astype(F32))
    picker = jnp.transpose(jnp.where(placed, 1.0, 0.0)).astype(BF16)
    mass_v[me] = jnp.sum(mass, axis=0, keepdims=True)

    slab_rows, packed_rows = GROUP * SLAB, segs * GROUP * CAP
    to_slab = one_hot(
        slab_place(iota((slab_rows, packed_rows), 0), segs) == iota((slab_rows, packed_rows), 1)
    )
    from_slab = one_hot(
        slab_place(iota((packed_rows, slab_rows), 1), segs) == iota((packed_rows, slab_rows), 0)
    )
    small[2].wait()
    tokens = tokens_v[...]
    for g in range(groups):
        rows = picker[g * GROUP * CAP : (g + 1) * GROUP * CAP]
        picked = dot(rows, tokens).astype(BF16)
        packed = jnp.concatenate([picked[:, s * seg_w : (s + 1) * seg_w] for s in range(segs)], axis=0)
        slabs = dot(to_slab, packed).astype(BF16)
        send_v[g * GROUP : (g + 1) * GROUP] = slabs.reshape(GROUP, SLAB, seg_w)

    def token_copy(d, src):
        return pltpu.make_async_remote_copy(
            src_ref=send_v.at[d], dst_ref=arrived_v.at[src],
            send_sem=send_sem.at[d], recv_sem=recv_sem.at[src],
            device_id={"exp": d}, device_id_type=MESH,
        )

    def mass_copy(d, src):
        return pltpu.make_async_remote_copy(
            src_ref=mass_v.at[me], dst_ref=mass_v.at[src],
            send_sem=mass_send_sem.at[d], recv_sem=mass_recv_sem.at[src],
            device_id={"exp": d}, device_id_type=MESH,
        )

    pl.semaphore_wait(barrier, n - 1)
    others(lambda d: token_copy(d, me).start())
    others(lambda d: mass_copy(d, me).start())
    arrived_v[me] = send_v[me]

    weights = jnp.where(placed, gates, 0.0)
    weights_hi = weights.astype(BF16)
    weights_lo = (weights - weights_hi.astype(F32)).astype(BF16)
    slab_lane = iota((lanes, slab_rows), 1)
    lane_seg = (iota((tok_rows, slab_rows), 1) % SLAB) // CAP
    for g in range(groups):
        slot_of = g * GROUP * CAP + slab_lane // SLAB * CAP + slab_lane % CAP
        spreading = one_hot(iota((lanes, slab_rows), 0) == slot_of)
        for part, term in enumerate((weights_hi, weights_lo)):
            wide = dot(term, spreading)
            for s in range(segs):
                mixing_v[
                    g, s * tok_rows : (s + 1) * tok_rows, part * slab_rows : (part + 1) * slab_rows
                ] = jnp.where(lane_seg == s, wide, 0.0).astype(BF16)

    others(lambda d: token_copy(d, d).wait_recv())
    for g in range(groups):
        slabs = arrived_v[g * GROUP : (g + 1) * GROUP].reshape(slab_rows, seg_w)
        packed = dot(from_slab, slabs).astype(BF16)
        for s in range(segs):
            x_v[s, g * GROUP * CAP : (g + 1) * GROUP * CAP] = packed[
                s * GROUP * CAP : (s + 1) * GROUP * CAP
            ]

    def gate_up(s, sums):
        gate_sum, up_sum = sums
        rows = x_v[s]
        gate_copy(s).wait()
        gate_sum = gate_sum + dot(rows, gate_v[s])
        up_copy(s).wait()
        up_sum = up_sum + dot(rows, up_v[s])
        return gate_sum, up_sum

    zero = jnp.zeros((n * CAP, k_parts * k_rows), F32)
    gate_sum, up_sum = lax.fori_loop(0, segs, gate_up, (zero, zero))
    hidden = (gate_sum / (1.0 + jnp.exp(-gate_sum)) * up_sum).astype(BF16)
    for k in range(k_parts):
        hidden_v[k] = hidden[:, k * k_rows : (k + 1) * k_rows]

    def back_copy(p, d, src):
        return pltpu.make_async_remote_copy(
            src_ref=back_v.at[p, d], dst_ref=returned_v.at[p, src],
            send_sem=back_send_sem.at[p, d], recv_sem=back_recv_sem.at[p, src],
            device_id={"exp": d}, device_id_type=MESH,
        )

    for p in range(pieces):

        def down(k, total, p=p):
            down_copy(p, k).wait()
            return total + dot(hidden_v[k], down_v[p * k_parts + k])

        total = lax.fori_loop(0, k_parts, down, jnp.zeros((n * CAP, piece_w), F32))
        partial_value = total.astype(BF16)
        for g in range(groups):
            rows = partial_value[g * GROUP * CAP : (g + 1) * GROUP * CAP]
            packed = jnp.concatenate(
                [rows[:, s * back_w : (s + 1) * back_w] for s in range(segs)], axis=0
            )
            slabs = dot(to_slab, packed).astype(BF16)
            back_v[p, g * GROUP : (g + 1) * GROUP] = slabs.reshape(GROUP, SLAB, back_w)
        others(lambda d, p=p: back_copy(p, d, me).start())
        returned_v[p, me] = back_v[p, me]

    others(lambda d: mass_copy(d, d).wait_recv())
    load_ref[...] = jnp.sum(mass_v[...], axis=0)

    for p in range(pieces):
        others(lambda d, p=p: back_copy(p, d, d).wait_recv())
        mixed = jnp.zeros((segs * tok_rows, back_w), F32)
        for g in range(groups):
            slabs = returned_v[p, g * GROUP : (g + 1) * GROUP].reshape(slab_rows, back_w)
            mixed = mixed + dot(mixing_v[g], jnp.concatenate([slabs, slabs], axis=0))
        for s in range(segs):
            low = p * piece_w + s * back_w
            out_ref[:, low : low + back_w] = mixed[s * tok_rows : (s + 1) * tok_rows].astype(BF16)

    others(lambda d: token_copy(d, d).wait_send())
    others(lambda d: mass_copy(d, d).wait_send())
    for p in range(pieces):
        others(lambda d, p=p: back_copy(p, d, d).wait_send())


def mixing_lanes(n):
    return -(-n * CAP // 128) * 128


def shards(tokens, expert_ids, gate_scores, gate_weight, up_weight, down_weight):
    n = lax.axis_size("exp")
    tok_rows, width = tokens.shape
    hid_dev = gate_weight.shape[1]
    spread = FF // hid_dev
    tiles = width // 128
    segs = max(s for s in range(1, SLAB // CAP + 1) if tiles % s == 0)
    seg_w = width // segs
    pieces = 2 if seg_w % 256 == 0 else 1
    piece_w = width // pieces
    k_parts = 4 if hid_dev % 512 == 0 else 1
    k_rows = hid_dev // k_parts
    groups = n // GROUP
    cfg = (n, spread, segs, seg_w, pieces, piece_w, k_parts, k_rows)
    dma = pltpu.SemaphoreType.DMA
    scratch = [
        pltpu.VMEM(tokens.shape, BF16),
        pltpu.VMEM(expert_ids.shape, jnp.int32),
        pltpu.VMEM(gate_scores.shape, F32),
        pltpu.VMEM((segs, seg_w, hid_dev), BF16),
        pltpu.VMEM((segs, seg_w, hid_dev), BF16),
        pltpu.VMEM((pieces * k_parts, k_rows, piece_w), BF16),
        pltpu.VMEM((n, SLAB, seg_w), BF16),
        pltpu.VMEM((n, SLAB, seg_w), BF16),
        pltpu.VMEM((segs, n * CAP, seg_w), BF16),
        pltpu.VMEM((pieces, n, SLAB, piece_w // segs), BF16),
        pltpu.VMEM((pieces, n, SLAB, piece_w // segs), BF16),
        pltpu.VMEM((n, 1, EXPERTS_ALL), F32),
        pltpu.VMEM((groups, segs * tok_rows, 2 * GROUP * SLAB), BF16),
        pltpu.VMEM((k_parts, n * CAP, k_rows), BF16),
        dma((3,)),
        dma((segs,)),
        dma((segs,)),
        dma((pieces * k_parts,)),
        dma((n,)),
        dma((n,)),
        dma((n,)),
        dma((n,)),
        dma((pieces, n)),
        dma((pieces, n)),
    ]
    combined, load = pl.pallas_call(
        functools.partial(kernel, cfg),
        out_shape=(
            jax.ShapeDtypeStruct(tokens.shape, BF16),
            jax.ShapeDtypeStruct((1, EXPERTS_ALL), F32),
        ),
        in_specs=[pl.BlockSpec(memory_space=pl.ANY)] * 6,
        out_specs=(pl.BlockSpec(memory_space=pltpu.VMEM), pl.BlockSpec(memory_space=pltpu.VMEM)),
        scratch_shapes=scratch,
        compiler_params=pltpu.CompilerParams(
            collective_id=0, has_side_effects=True, vmem_limit_bytes=56 * 1024 * 1024
        ),
    )(tokens, expert_ids, gate_scores, gate_weight, up_weight, down_weight)
    return (combined, load.reshape(EXPERTS_ALL))


def solution(mesh):
    return jax.shard_map(
        shards,
        mesh=mesh,
        in_specs=(
            P(("rep", "exp"), None),
            P(("rep", "exp"), None),
            P(("rep", "exp"), None),
            P(None, "exp"),
            P(None, "exp"),
            P("exp", None),
        ),
        out_specs=(P(("rep", "exp"), None), P("rep")),
        check_vma=False,
    )
```

```python
import functools

import jax
import jax.numpy as jnp
from jax import lax
from jax.experimental import pallas as pl
from jax.experimental.pallas import tpu as pltpu
from jax.sharding import PartitionSpec as P

FF = 2048
EXPERTS_ALL = 384
CAP = 2
SLAB = 16
GROUP = 8
TILE = 256
MESH = pl.DeviceIdType.MESH
BF16 = jnp.bfloat16
F32 = jnp.float32


def dot(a, b):
    return jnp.dot(a, b, preferred_element_type=F32)


def iota(shape, dim):
    return lax.broadcasted_iota(jnp.int32, shape, dim)


def one_hot(mask):
    return jnp.where(mask, 1.0, 0.0).astype(BF16)


def slab_place(i, segs):
    dev, seg, row = i // SLAB, (i % SLAB) // CAP, i % CAP
    return jnp.where(seg < segs, seg * (GROUP * CAP) + dev * CAP + row, -1)


def kernel(
    cfg,
    tokens_hbm, ids_hbm, scores_hbm, gate_hbm, up_hbm, down_hbm,
    out_ref, load_ref,
    tokens_v, ids_v, scores_v, gate_v, up_v, down_v,
    send_v, arrived_v, back_v, returned_v, mass_v, mixing_v, x_v, gate_sum, up_sum, hidden_v,
    small_sem, gate_sem, up_sem, down_sem,
    send_sem, recv_sem, mass_send_sem, mass_recv_sem, back_send_sem, back_recv_sem,
):
    n, spread, segs, pieces, piece_w, seg_w = cfg
    groups = n // GROUP
    top, tok_rows = ids_v.shape
    lanes = mixing_lanes(n)
    me = lax.axis_index("exp")

    small = [
        pltpu.make_async_copy(ids_hbm, ids_v, small_sem.at[0]),
        pltpu.make_async_copy(scores_hbm, scores_v, small_sem.at[1]),
        pltpu.make_async_copy(tokens_hbm, tokens_v, small_sem.at[2]),
    ]
    for copy in small:
        copy.start()

    def gate_copy(p):
        return pltpu.make_async_copy(
            gate_hbm.at[pl.ds(p * piece_w, piece_w), :], gate_v.at[p], gate_sem.at[p]
        )

    def up_copy(p):
        return pltpu.make_async_copy(
            up_hbm.at[pl.ds(p * piece_w, piece_w), :], up_v.at[p], up_sem.at[p]
        )

    def down_copy(p):
        return pltpu.make_async_copy(
            down_hbm.at[:, pl.ds(p * piece_w, piece_w)], down_v.at[p], down_sem.at[p]
        )

    for p in range(pieces):
        gate_copy(p).start()
        up_copy(p).start()
    for p in range(pieces):
        down_copy(p).start()

    def others(body):
        def step(i, carry):
            body(lax.rem(me + i, n))
            return carry

        lax.fori_loop(1, n, step, 0, unroll=n <= 16)

    barrier = pltpu.get_barrier_semaphore()
    others(lambda d: pl.semaphore_signal(barrier, inc=1, device_id={"exp": d}, device_id_type=MESH))

    for copy in small[:2]:
        copy.wait()
    ids = jnp.transpose(ids_v[...])
    scores = jnp.transpose(scores_v[...])
    all_ids = iota((tok_rows, EXPERTS_ALL), 1)
    slot = iota((tok_rows, lanes), 1)
    slot_expert = jnp.where(slot < n * CAP, slot // (CAP * spread), -1)
    mass = jnp.zeros((tok_rows, EXPERTS_ALL), F32)
    gates = jnp.zeros((tok_rows, lanes), F32)
    hits = jnp.zeros((tok_rows, lanes), F32)
    for k in range(top):
        id_k, score_k = ids[:, k : k + 1], scores[:, k : k + 1]
        mass = mass + jnp.where(id_k == all_ids, score_k, 0.0)
        found = id_k == slot_expert
        gates = gates + jnp.where(found, score_k, 0.0)
        hits = hits + jnp.where(found, 1.0, 0.0)
    earlier = one_hot(iota((tok_rows, tok_rows), 1) < iota((tok_rows, tok_rows), 0))
    position = dot(earlier, hits.astype(BF16))
    placed = (hits > 0.5) & (position == (slot % CAP).astype(F32))
    picker = jnp.transpose(jnp.where(placed, 1.0, 0.0)).astype(BF16)
    mass_v[me] = jnp.sum(mass, axis=0, keepdims=True)

    slab_rows, packed_rows = GROUP * SLAB, segs * GROUP * CAP
    to_slab = one_hot(
        slab_place(iota((slab_rows, packed_rows), 0), segs) == iota((slab_rows, packed_rows), 1)
    )
    from_slab = one_hot(
        slab_place(iota((packed_rows, slab_rows), 1), segs) == iota((packed_rows, slab_rows), 0)
    )

    def pack(rows):
        packed = jnp.concatenate([rows[:, s * seg_w : (s + 1) * seg_w] for s in range(segs)], axis=0)
        return dot(to_slab, packed).astype(BF16).reshape(GROUP, SLAB, seg_w)

    small[2].wait()
    tokens = tokens_v[...]
    for g in range(groups):
        rows = picker[g * GROUP * CAP : (g + 1) * GROUP * CAP]
        picked = dot(rows, tokens).astype(BF16)
        for p in range(pieces):
            slabs = pack(picked[:, p * piece_w : (p + 1) * piece_w])
            send_v[p, g * GROUP : (g + 1) * GROUP] = slabs

    def token_copy(p, d, src):
        return pltpu.make_async_remote_copy(
            src_ref=send_v.at[p, d], dst_ref=arrived_v.at[p, src],
            send_sem=send_sem.at[p, d], recv_sem=recv_sem.at[p, src],
            device_id={"exp": d}, device_id_type=MESH,
        )

    def mass_copy(d, src):
        return pltpu.make_async_remote_copy(
            src_ref=mass_v.at[me], dst_ref=mass_v.at[src],
            send_sem=mass_send_sem.at[d], recv_sem=mass_recv_sem.at[src],
            device_id={"exp": d}, device_id_type=MESH,
        )

    pl.semaphore_wait(barrier, n - 1)
    for p in range(pieces):
        others(lambda d, p=p: token_copy(p, d, me).start())
        arrived_v[p, me] = send_v[p, me]
    others(lambda d: mass_copy(d, me).start())

    weights = jnp.where(placed, gates, 0.0)
    weights_hi = weights.astype(BF16)
    weights_lo = (weights - weights_hi.astype(F32)).astype(BF16)
    slab_lane = iota((lanes, slab_rows), 1)
    lane_seg = (iota((tok_rows, slab_rows), 1) % SLAB) // CAP
    for g in range(groups):
        slot_of = g * GROUP * CAP + slab_lane // SLAB * CAP + slab_lane % CAP
        spreading = one_hot(iota((lanes, slab_rows), 0) == slot_of)
        for part, term in enumerate((weights_hi, weights_lo)):
            wide = dot(term, spreading)
            for s in range(segs):
                mixing_v[
                    g, s * tok_rows : (s + 1) * tok_rows, part * slab_rows : (part + 1) * slab_rows
                ] = jnp.where(lane_seg == s, wide, 0.0).astype(BF16)

    hid_dev = hidden_v.shape[1]
    hid_tile = min(TILE, hid_dev)
    for p in range(pieces):
        others(lambda d, p=p: token_copy(p, d, d).wait_recv())
        for g in range(groups):
            slabs = arrived_v[p, g * GROUP : (g + 1) * GROUP].reshape(slab_rows, seg_w)
            packed = dot(from_slab, slabs).astype(BF16)
            size = GROUP * CAP
            for s in range(segs):
                x_v[g * size : (g + 1) * size, s * seg_w : (s + 1) * seg_w] = packed[
                    s * size : (s + 1) * size
                ]
        gate_copy(p).wait()
        up_copy(p).wait()

        def gate_up(j, carry, p=p):
            cols = pl.ds(pl.multiple_of(j * hid_tile, hid_tile), hid_tile)
            gate_act = dot(x_v[...], gate_v[p, :, cols])
            up_act = dot(x_v[...], up_v[p, :, cols])
            if p > 0:
                gate_act = gate_act + gate_sum[:, cols]
                up_act = up_act + up_sum[:, cols]
            if p < pieces - 1:
                gate_sum[:, cols] = gate_act
                up_sum[:, cols] = up_act
            else:
                silu = gate_act / (1.0 + jnp.exp(-gate_act))
                hidden_v[:, cols] = (silu * up_act).astype(BF16)
            return carry

        lax.fori_loop(0, hid_dev // hid_tile, gate_up, 0)

    def back_copy(p, d, src):
        return pltpu.make_async_remote_copy(
            src_ref=back_v.at[p, d], dst_ref=returned_v.at[p, src],
            send_sem=back_send_sem.at[p, d], recv_sem=back_recv_sem.at[p, src],
            device_id={"exp": d}, device_id_type=MESH,
        )

    for p in range(pieces):
        down_copy(p).wait()
        for s in range(segs):
            cols = slice(s * seg_w, (s + 1) * seg_w)
            x_v[:, cols] = dot(hidden_v[...], down_v[p, :, cols]).astype(BF16)
        for g in range(groups):
            rows = x_v[g * GROUP * CAP : (g + 1) * GROUP * CAP]
            back_v[p, g * GROUP : (g + 1) * GROUP] = pack(rows)
        others(lambda d, p=p: back_copy(p, d, me).start())
        returned_v[p, me] = back_v[p, me]

    others(lambda d: mass_copy(d, d).wait_recv())
    load_ref[...] = jnp.sum(mass_v[...], axis=0).reshape(EXPERTS_ALL)

    for p in range(pieces):
        others(lambda d, p=p: back_copy(p, d, d).wait_recv())
        mixed = jnp.zeros((segs * tok_rows, seg_w), F32)
        for g in range(groups):
            slabs = returned_v[p, g * GROUP : (g + 1) * GROUP].reshape(slab_rows, seg_w)
            mixed = mixed + dot(mixing_v[g], jnp.concatenate([slabs, slabs], axis=0))
        for s in range(segs):
            low = p * piece_w + s * seg_w
            out_ref[:, low : low + seg_w] = mixed[s * tok_rows : (s + 1) * tok_rows].astype(BF16)

    others(lambda d: mass_copy(d, d).wait_send())
    for p in range(pieces):
        others(lambda d, p=p: token_copy(p, d, d).wait_send())
        others(lambda d, p=p: back_copy(p, d, d).wait_send())


def mixing_lanes(n):
    return -(-n * CAP // 128) * 128


def copy_out(combined_in, load_in, combined_out, load_out, sem):
    copies = [
        pltpu.make_async_copy(combined_in, combined_out, sem.at[0]),
        pltpu.make_async_copy(load_in, load_out, sem.at[1]),
    ]
    for copy in copies:
        copy.start()
    for copy in copies:
        copy.wait()


def shards(tokens, expert_ids, gate_scores, gate_weight, up_weight, down_weight):
    n = lax.axis_size("exp")
    tok_rows, width = tokens.shape
    hid_dev = gate_weight.shape[1]
    spread = FF // hid_dev
    tiles = width // 128
    segs = max(s for s in range(1, SLAB // CAP + 1) if tiles % s == 0)
    pieces = 2 if tiles % (2 * segs) == 0 else 1
    piece_w = width // pieces
    seg_w = piece_w // segs
    groups = n // GROUP
    cfg = (n, spread, segs, pieces, piece_w, seg_w)
    dma = pltpu.SemaphoreType.DMA
    scratch = [
        pltpu.VMEM(tokens.shape, BF16),
        pltpu.VMEM(expert_ids.shape[::-1], jnp.int32),
        pltpu.VMEM(gate_scores.shape[::-1], F32),
        pltpu.VMEM((pieces, piece_w, hid_dev), BF16),
        pltpu.VMEM((pieces, piece_w, hid_dev), BF16),
        pltpu.VMEM((pieces, hid_dev, piece_w), BF16),
        pltpu.VMEM((pieces, n, SLAB, seg_w), BF16),
        pltpu.VMEM((pieces, n, SLAB, seg_w), BF16),
        pltpu.VMEM((pieces, n, SLAB, seg_w), BF16),
        pltpu.VMEM((pieces, n, SLAB, seg_w), BF16),
        pltpu.VMEM((n, 1, EXPERTS_ALL), F32),
        pltpu.VMEM((groups, segs * tok_rows, 2 * GROUP * SLAB), BF16),
        pltpu.VMEM((n * CAP, piece_w), BF16),
        pltpu.VMEM((n * CAP, hid_dev), F32),
        pltpu.VMEM((n * CAP, hid_dev), F32),
        pltpu.VMEM((n * CAP, hid_dev), BF16),
        dma((3,)),
        dma((pieces,)),
        dma((pieces,)),
        dma((pieces,)),
        dma((pieces, n)),
        dma((pieces, n)),
        dma((n,)),
        dma((n,)),
        dma((pieces, n)),
        dma((pieces, n)),
    ]
    anywhere = pl.BlockSpec(memory_space=pl.ANY)
    out_shape = (
        jax.ShapeDtypeStruct(tokens.shape, BF16),
        jax.ShapeDtypeStruct((EXPERTS_ALL,), F32),
    )
    combined, load = pl.pallas_call(
        functools.partial(kernel, cfg),
        out_shape=out_shape,
        in_specs=[pl.BlockSpec(memory_space=pltpu.HBM)] * 6,
        out_specs=(pl.BlockSpec(memory_space=pltpu.VMEM), pl.BlockSpec(memory_space=pltpu.VMEM)),
        scratch_shapes=scratch,
        compiler_params=pltpu.CompilerParams(
            collective_id=0, has_side_effects=True, vmem_limit_bytes=62 * 1024 * 1024
        ),
    )(tokens, expert_ids.T, gate_scores.T, gate_weight, up_weight, down_weight)
    return pl.pallas_call(
        copy_out,
        out_shape=out_shape,
        in_specs=[anywhere] * 2,
        out_specs=(anywhere, anywhere),
        scratch_shapes=[dma((2,))],
    )(combined, load)


def solution(mesh):
    return jax.shard_map(
        shards,
        mesh=mesh,
        in_specs=(
            P(("rep", "exp"), None),
            P(("rep", "exp"), None),
            P(("rep", "exp"), None),
            P(None, "exp"),
            P(None, "exp"),
            P("exp", None),
        ),
        out_specs=(P(("rep", "exp"), None), P("rep")),
        check_vma=False,
    )
```

```python
import functools

import jax
import jax.numpy as jnp
from jax import lax
from jax.experimental import pallas as pl
from jax.experimental.pallas import tpu as pltpu
from jax.sharding import PartitionSpec as P

FF = 2048
EXPERTS_ALL = 384
CAP = 2
SLAB = 16
GROUP = 8
TILE = 256
MESH = pl.DeviceIdType.MESH
BF16 = jnp.bfloat16
F32 = jnp.float32


def dot(a, b):
    return jnp.dot(a, b, preferred_element_type=F32)


def iota(shape, dim):
    return lax.broadcasted_iota(jnp.int32, shape, dim)


def one_hot(mask):
    return jnp.where(mask, 1.0, 0.0).astype(BF16)


def slab_place(i, segs):
    dev, seg, row = i // SLAB, (i % SLAB) // CAP, i % CAP
    return jnp.where(seg < segs, seg * (GROUP * CAP) + dev * CAP + row, -1)


def kernel(
    cfg,
    tokens_hbm, ids_hbm, scores_hbm, gate_hbm, up_hbm, down_hbm,
    out_ref, load_ref,
    tokens_v, ids_v, scores_v, gate_v, up_v, down_v,
    send_v, arrived_v, back_v, returned_v, mass_v, mixing_v, x_v, gate_sum, up_sum, hidden_v,
    small_sem, gate_sem, up_sem, down_sem,
    send_sem, recv_sem, mass_send_sem, mass_recv_sem, back_send_sem, back_recv_sem,
):
    n, spread, segs, pieces, piece_w, seg_w = cfg
    groups = n // GROUP
    top, tok_rows = ids_v.shape
    lanes = mixing_lanes(n)
    me = lax.axis_index("exp")

    small = [
        pltpu.make_async_copy(ids_hbm, ids_v, small_sem.at[0]),
        pltpu.make_async_copy(scores_hbm, scores_v, small_sem.at[1]),
        pltpu.make_async_copy(tokens_hbm, tokens_v, small_sem.at[2]),
    ]
    for copy in small:
        copy.start()

    def gate_copy(p):
        return pltpu.make_async_copy(
            gate_hbm.at[pl.ds(p * piece_w, piece_w), :], gate_v.at[p], gate_sem.at[p]
        )

    def up_copy(p):
        return pltpu.make_async_copy(
            up_hbm.at[pl.ds(p * piece_w, piece_w), :], up_v.at[p], up_sem.at[p]
        )

    def down_copy(p):
        return pltpu.make_async_copy(
            down_hbm.at[:, pl.ds(p * piece_w, piece_w)], down_v.at[p], down_sem.at[p]
        )

    gate_copy(0).start()
    up_copy(0).start()

    def others(body):
        def step(i, carry):
            body(lax.rem(me + i, n))
            return carry

        lax.fori_loop(1, n, step, 0, unroll=n <= 16)

    barrier = pltpu.get_barrier_semaphore()
    others(lambda d: pl.semaphore_signal(barrier, inc=1, device_id={"exp": d}, device_id_type=MESH))

    for copy in small[:2]:
        copy.wait()
    ids = jnp.transpose(ids_v[...])
    scores = jnp.transpose(scores_v[...])
    all_ids = iota((tok_rows, EXPERTS_ALL), 1)
    slot = iota((tok_rows, lanes), 1)
    slot_expert = jnp.where(slot < n * CAP, slot // (CAP * spread), -1)
    mass = jnp.zeros((tok_rows, EXPERTS_ALL), F32)
    gates = jnp.zeros((tok_rows, lanes), F32)
    hits = jnp.zeros((tok_rows, lanes), F32)
    for k in range(top):
        id_k, score_k = ids[:, k : k + 1], scores[:, k : k + 1]
        mass = mass + jnp.where(id_k == all_ids, score_k, 0.0)
        found = id_k == slot_expert
        gates = gates + jnp.where(found, score_k, 0.0)
        hits = hits + jnp.where(found, 1.0, 0.0)
    earlier = one_hot(iota((tok_rows, tok_rows), 1) < iota((tok_rows, tok_rows), 0))
    position = dot(earlier, hits.astype(BF16))
    placed = (hits > 0.5) & (position == (slot % CAP).astype(F32))
    picker = jnp.transpose(jnp.where(placed, 1.0, 0.0)).astype(BF16)
    mass_v[me] = jnp.sum(mass, axis=0, keepdims=True)

    slab_rows, packed_rows = GROUP * SLAB, segs * GROUP * CAP
    to_slab = one_hot(
        slab_place(iota((slab_rows, packed_rows), 0), segs) == iota((slab_rows, packed_rows), 1)
    )
    from_slab = one_hot(
        slab_place(iota((packed_rows, slab_rows), 1), segs) == iota((packed_rows, slab_rows), 0)
    )

    def pack(rows):
        packed = jnp.concatenate([rows[:, s * seg_w : (s + 1) * seg_w] for s in range(segs)], axis=0)
        return dot(to_slab, packed).astype(BF16).reshape(GROUP, SLAB, seg_w)

    small[2].wait()
    tokens = tokens_v[...]
    for g in range(groups):
        rows = picker[g * GROUP * CAP : (g + 1) * GROUP * CAP]
        picked = dot(rows, tokens).astype(BF16)
        for p in range(pieces):
            slabs = pack(picked[:, p * piece_w : (p + 1) * piece_w])
            send_v[p, g * GROUP : (g + 1) * GROUP] = slabs

    def token_copy(p, d, src):
        return pltpu.make_async_remote_copy(
            src_ref=send_v.at[p, d], dst_ref=arrived_v.at[p, src],
            send_sem=send_sem.at[p, d], recv_sem=recv_sem.at[p, src],
            device_id={"exp": d}, device_id_type=MESH,
        )

    def mass_copy(d, src):
        return pltpu.make_async_remote_copy(
            src_ref=mass_v.at[me], dst_ref=mass_v.at[src],
            send_sem=mass_send_sem.at[d], recv_sem=mass_recv_sem.at[src],
            device_id={"exp": d}, device_id_type=MESH,
        )

    pl.semaphore_wait(barrier, n - 1)
    for p in range(pieces):
        others(lambda d, p=p: token_copy(p, d, me).start())
        arrived_v[p, me] = send_v[p, me]
    for p in range(1, pieces):
        gate_copy(p).start()
        up_copy(p).start()
    for p in range(pieces):
        down_copy(p).start()
    others(lambda d: mass_copy(d, me).start())

    weights = jnp.where(placed, gates, 0.0)
    weights_hi = weights.astype(BF16)
    weights_lo = (weights - weights_hi.astype(F32)).astype(BF16)
    slab_lane = iota((lanes, slab_rows), 1)
    lane_seg = (iota((tok_rows, slab_rows), 1) % SLAB) // CAP
    for g in range(groups):
        slot_of = g * GROUP * CAP + slab_lane // SLAB * CAP + slab_lane % CAP
        spreading = one_hot(iota((lanes, slab_rows), 0) == slot_of)
        for part, term in enumerate((weights_hi, weights_lo)):
            wide = dot(term, spreading)
            for s in range(segs):
                mixing_v[
                    g, s * tok_rows : (s + 1) * tok_rows, part * slab_rows : (part + 1) * slab_rows
                ] = jnp.where(lane_seg == s, wide, 0.0).astype(BF16)

    hid_dev = hidden_v.shape[1]
    hid_tile = min(TILE, hid_dev)
    for p in range(pieces):
        others(lambda d, p=p: token_copy(p, d, d).wait_recv())
        for g in range(groups):
            slabs = arrived_v[p, g * GROUP : (g + 1) * GROUP].reshape(slab_rows, seg_w)
            packed = dot(from_slab, slabs).astype(BF16)
            size = GROUP * CAP
            for s in range(segs):
                x_v[g * size : (g + 1) * size, s * seg_w : (s + 1) * seg_w] = packed[
                    s * size : (s + 1) * size
                ]
        gate_copy(p).wait()
        up_copy(p).wait()

        def gate_up(j, carry, p=p):
            cols = pl.ds(pl.multiple_of(j * hid_tile, hid_tile), hid_tile)
            gate_act = dot(x_v[...], gate_v[p, :, cols])
            up_act = dot(x_v[...], up_v[p, :, cols])
            if p > 0:
                gate_act = gate_act + gate_sum[:, cols]
                up_act = up_act + up_sum[:, cols]
            if p < pieces - 1:
                gate_sum[:, cols] = gate_act
                up_sum[:, cols] = up_act
            else:
                silu = gate_act / (1.0 + jnp.exp(-gate_act))
                hidden_v[:, cols] = (silu * up_act).astype(BF16)
            return carry

        lax.fori_loop(0, hid_dev // hid_tile, gate_up, 0)

    def back_copy(p, d, src):
        return pltpu.make_async_remote_copy(
            src_ref=back_v.at[p, d], dst_ref=returned_v.at[p, src],
            send_sem=back_send_sem.at[p, d], recv_sem=back_recv_sem.at[p, src],
            device_id={"exp": d}, device_id_type=MESH,
        )

    for p in range(pieces):
        down_copy(p).wait()
        for s in range(segs):
            cols = slice(s * seg_w, (s + 1) * seg_w)
            x_v[:, cols] = dot(hidden_v[...], down_v[p, :, cols]).astype(BF16)
        for g in range(groups):
            rows = x_v[g * GROUP * CAP : (g + 1) * GROUP * CAP]
            back_v[p, g * GROUP : (g + 1) * GROUP] = pack(rows)
        others(lambda d, p=p: back_copy(p, d, me).start())
        returned_v[p, me] = back_v[p, me]

    others(lambda d: mass_copy(d, d).wait_recv())
    load_ref[...] = jnp.sum(mass_v[...], axis=0).reshape(EXPERTS_ALL)

    for p in range(pieces):
        others(lambda d, p=p: back_copy(p, d, d).wait_recv())
        mixed = jnp.zeros((segs * tok_rows, seg_w), F32)
        for g in range(groups):
            slabs = returned_v[p, g * GROUP : (g + 1) * GROUP].reshape(slab_rows, seg_w)
            mixed = mixed + dot(mixing_v[g], jnp.concatenate([slabs, slabs], axis=0))
        for s in range(segs):
            low = p * piece_w + s * seg_w
            out_ref[:, low : low + seg_w] = mixed[s * tok_rows : (s + 1) * tok_rows].astype(BF16)

    others(lambda d: mass_copy(d, d).wait_send())
    for p in range(pieces):
        others(lambda d, p=p: token_copy(p, d, d).wait_send())
        others(lambda d, p=p: back_copy(p, d, d).wait_send())


def mixing_lanes(n):
    return -(-n * CAP // 128) * 128


def copy_out(combined_in, load_in, combined_out, load_out):
    combined_out[...] = combined_in[...]
    load_out[...] = load_in[...]


def shards(tokens, expert_ids, gate_scores, gate_weight, up_weight, down_weight):
    n = lax.axis_size("exp")
    tok_rows, width = tokens.shape
    hid_dev = gate_weight.shape[1]
    spread = FF // hid_dev
    tiles = width // 128
    segs = max(s for s in range(1, SLAB // CAP + 1) if tiles % s == 0)
    pieces = 2 if tiles % (2 * segs) == 0 else 1
    piece_w = width // pieces
    seg_w = piece_w // segs
    groups = n // GROUP
    cfg = (n, spread, segs, pieces, piece_w, seg_w)
    dma = pltpu.SemaphoreType.DMA
    scratch = [
        pltpu.VMEM(tokens.shape, BF16),
        pltpu.VMEM(expert_ids.shape[::-1], jnp.int32),
        pltpu.VMEM(gate_scores.shape[::-1], F32),
        pltpu.VMEM((pieces, piece_w, hid_dev), BF16),
        pltpu.VMEM((pieces, piece_w, hid_dev), BF16),
        pltpu.VMEM((pieces, hid_dev, piece_w), BF16),
        pltpu.VMEM((pieces, n, SLAB, seg_w), BF16),
        pltpu.VMEM((pieces, n, SLAB, seg_w), BF16),
        pltpu.VMEM((pieces, n, SLAB, seg_w), BF16),
        pltpu.VMEM((pieces, n, SLAB, seg_w), BF16),
        pltpu.VMEM((n, 1, EXPERTS_ALL), F32),
        pltpu.VMEM((groups, segs * tok_rows, 2 * GROUP * SLAB), BF16),
        pltpu.VMEM((n * CAP, piece_w), BF16),
        pltpu.VMEM((n * CAP, hid_dev), F32),
        pltpu.VMEM((n * CAP, hid_dev), F32),
        pltpu.VMEM((n * CAP, hid_dev), BF16),
        dma((3,)),
        dma((pieces,)),
        dma((pieces,)),
        dma((pieces,)),
        dma((pieces, n)),
        dma((pieces, n)),
        dma((n,)),
        dma((n,)),
        dma((pieces, n)),
        dma((pieces, n)),
    ]
    vmem = pl.BlockSpec(memory_space=pltpu.VMEM)
    out_shape = (
        jax.ShapeDtypeStruct(tokens.shape, BF16),
        jax.ShapeDtypeStruct((EXPERTS_ALL,), F32),
    )
    combined, load = pl.pallas_call(
        functools.partial(kernel, cfg),
        out_shape=out_shape,
        in_specs=[pl.BlockSpec(memory_space=pltpu.HBM)] * 6,
        out_specs=(vmem, vmem),
        scratch_shapes=scratch,
        compiler_params=pltpu.CompilerParams(
            collective_id=0, has_side_effects=True, vmem_limit_bytes=62 * 1024 * 1024
        ),
    )(tokens, expert_ids.T, gate_scores.T, gate_weight, up_weight, down_weight)
    return pl.pallas_call(
        copy_out,
        out_shape=out_shape,
        in_specs=[vmem, vmem],
        out_specs=(vmem, vmem),
    )(combined, load)


def solution(mesh):
    return jax.shard_map(
        shards,
        mesh=mesh,
        in_specs=(
            P(("rep", "exp"), None),
            P(("rep", "exp"), None),
            P(("rep", "exp"), None),
            P(None, "exp"),
            P(None, "exp"),
            P("exp", None),
        ),
        out_specs=(P(("rep", "exp"), None), P("rep")),
        check_vma=False,
    )
```

```python
import functools

import jax
import jax.numpy as jnp
from jax import lax
from jax.experimental import pallas as pl
from jax.experimental.pallas import tpu as pltpu
from jax.sharding import PartitionSpec as P

FF = 2048
EXPERTS_ALL = 384
CAP = 2
SLAB = 16
GROUP = 8
SEGS = SLAB // CAP
LANES = 128
TILE = 256
MESH = pl.DeviceIdType.MESH
BF16 = jnp.bfloat16
F32 = jnp.float32


def dot(a, b):
    return jnp.dot(a, b, preferred_element_type=F32)


def iota(shape, dim):
    return lax.broadcasted_iota(jnp.int32, shape, dim)


def one_hot(mask):
    return jnp.where(mask, 1.0, 0.0).astype(BF16)


def slab_place(i):
    dev, seg, row = i // SLAB, (i % SLAB) // CAP, i % CAP
    return seg * (GROUP * CAP) + dev * CAP + row


def cut(width):
    pieces, low, lane = [], 0, 0
    while low < width:
        seg_w = 2 * LANES if width - low >= 2 * LANES * SEGS else LANES
        segs = min(SEGS, (width - low) // seg_w)
        pieces.append((low, lane, segs, seg_w))
        low, lane = low + segs * seg_w, lane + seg_w
    return pieces


def kernel(
    cfg,
    tokens_hbm, ids_hbm, scores_hbm, gate_hbm, up_hbm, down_hbm,
    returned_hbm, mixing_hbm, load_hbm,
    tokens_v, ids_v, scores_v, gate_v, up_v, down_v,
    send_v, arrived_v, back_v, mass_v, load_v, mixing_v, x_v, gate_sum, up_sum, hidden_v,
    small_sem, gate_sem, up_sem, down_sem, out_sem, own_sem,
    send_sem, recv_sem, mass_send_sem, mass_recv_sem, back_send_sem, back_recv_sem,
):
    n, spread, pieces = cfg
    groups = n // GROUP
    top, tok_rows = ids_v.shape
    lanes = mixing_lanes(n)
    me = lax.axis_index("exp")
    forward = list(enumerate(pieces))
    backward = forward[::-1]

    small = [
        pltpu.make_async_copy(ids_hbm, ids_v, small_sem.at[0]),
        pltpu.make_async_copy(scores_hbm, scores_v, small_sem.at[1]),
        pltpu.make_async_copy(tokens_hbm, tokens_v, small_sem.at[2]),
    ]
    for copy in small:
        copy.start()

    def columns(piece):
        low, _, segs, seg_w = piece
        return pl.ds(low, segs * seg_w)

    def gate_copy(p):
        rows = columns(pieces[p])
        return pltpu.make_async_copy(gate_hbm.at[rows, :], gate_v.at[rows, :], gate_sem.at[p])

    def up_copy(p):
        rows = columns(pieces[p])
        return pltpu.make_async_copy(up_hbm.at[rows, :], up_v.at[rows, :], up_sem.at[p])

    def down_copy(p):
        cols = columns(pieces[p])
        return pltpu.make_async_copy(down_hbm.at[:, cols], down_v.at[:, cols], down_sem.at[p])

    for p, _ in backward[:-1]:
        gate_copy(p).start()
        up_copy(p).start()

    def others(body):
        def step(i, carry):
            body(lax.rem(me + i, n))
            return carry

        lax.fori_loop(1, n, step, 0, unroll=n <= 16)

    barrier = pltpu.get_barrier_semaphore()
    others(lambda d: pl.semaphore_signal(barrier, inc=1, device_id={"exp": d}, device_id_type=MESH))

    for copy in small[:2]:
        copy.wait()
    ids = jnp.transpose(ids_v[...])
    scores = jnp.transpose(scores_v[...])
    all_ids = iota((tok_rows, EXPERTS_ALL), 1)
    slot = iota((tok_rows, lanes), 1)
    slot_expert = jnp.where(slot < n * CAP, slot // (CAP * spread), -1)
    mass = jnp.zeros((tok_rows, EXPERTS_ALL), F32)
    gates = jnp.zeros((tok_rows, lanes), F32)
    hits = jnp.zeros((tok_rows, lanes), F32)
    for k in range(top):
        id_k, score_k = ids[:, k : k + 1], scores[:, k : k + 1]
        mass = mass + jnp.where(id_k == all_ids, score_k, 0.0)
        found = id_k == slot_expert
        gates = gates + jnp.where(found, score_k, 0.0)
        hits = hits + jnp.where(found, 1.0, 0.0)
    earlier = one_hot(iota((tok_rows, tok_rows), 1) < iota((tok_rows, tok_rows), 0))
    position = dot(earlier, hits.astype(BF16))
    placed = (hits > 0.5) & (position == (slot % CAP).astype(F32))
    picker = jnp.transpose(jnp.where(placed, 1.0, 0.0)).astype(BF16)
    mass_v[me] = jnp.sum(mass, axis=0, keepdims=True)

    slab_rows = GROUP * SLAB
    square = (slab_rows, slab_rows)
    to_slab = one_hot(slab_place(iota(square, 0)) == iota(square, 1))
    from_slab = one_hot(slab_place(iota(square, 1)) == iota(square, 0))

    def pack(rows, piece):
        _, _, segs, seg_w = piece
        parts = [rows[:, s * seg_w : (s + 1) * seg_w] for s in range(segs)]
        parts += [jnp.zeros_like(parts[0])] * (SEGS - segs)
        packed = jnp.concatenate(parts, axis=0)
        return dot(to_slab, packed).astype(BF16).reshape(GROUP, SLAB, seg_w)

    def slab_lanes(piece):
        return slice(piece[1], piece[1] + piece[3])

    small[2].wait()
    tokens = tokens_v[...]
    for g in range(groups):
        rows = picker[g * GROUP * CAP : (g + 1) * GROUP * CAP]
        picked = dot(rows, tokens).astype(BF16)
        for p, piece in backward:
            low, _, segs, seg_w = piece
            send_v[g * GROUP : (g + 1) * GROUP, :, slab_lanes(piece)] = pack(
                picked[:, low : low + segs * seg_w], piece
            )

    def token_copy(p, d, src):
        at = pl.ds(pieces[p][1], pieces[p][3])
        return pltpu.make_async_remote_copy(
            src_ref=send_v.at[d, :, at], dst_ref=arrived_v.at[src, :, at],
            send_sem=send_sem.at[p, d], recv_sem=recv_sem.at[p, src],
            device_id={"exp": d}, device_id_type=MESH,
        )

    def mass_copy(d, src):
        return pltpu.make_async_remote_copy(
            src_ref=mass_v.at[me], dst_ref=mass_v.at[src],
            send_sem=mass_send_sem.at[d], recv_sem=mass_recv_sem.at[src],
            device_id={"exp": d}, device_id_type=MESH,
        )

    pl.semaphore_wait(barrier, n - 1)
    for p, _ in backward:
        others(lambda d, p=p: token_copy(p, d, me).start())
    arrived_v[me] = send_v[me]
    gate_copy(0).start()
    up_copy(0).start()
    for p, _ in forward:
        down_copy(p).start()
    others(lambda d: mass_copy(d, me).start())

    weights = jnp.where(placed, gates, 0.0)
    weights_hi = weights.astype(BF16)
    weights_lo = (weights - weights_hi.astype(F32)).astype(BF16)
    slab_lane = iota((lanes, slab_rows), 1)
    lane_seg = (iota((tok_rows, slab_rows), 1) % SLAB) // CAP
    for g in range(groups):
        slot_of = g * GROUP * CAP + slab_lane // SLAB * CAP + slab_lane % CAP
        spreading = one_hot(iota((lanes, slab_rows), 0) == slot_of)
        for part, term in enumerate((weights_hi, weights_lo)):
            wide = dot(term, spreading)
            for s in range(SEGS):
                mixing_v[
                    g, s * tok_rows : (s + 1) * tok_rows, part * slab_rows : (part + 1) * slab_rows
                ] = jnp.where(lane_seg == s, wide, 0.0).astype(BF16)

    mixing_out = pltpu.make_async_copy(mixing_v, mixing_hbm, out_sem.at[0])
    mixing_out.start()

    hid_dev = hidden_v.shape[1]
    hid_tile = min(TILE, hid_dev)
    for p, piece in backward:
        low, _, segs, seg_w = piece
        at = slice(low, low + segs * seg_w)
        others(lambda d, p=p: token_copy(p, d, d).wait_recv())
        for g in range(groups):
            slabs = arrived_v[g * GROUP : (g + 1) * GROUP, :, slab_lanes(piece)]
            packed = dot(from_slab, slabs.reshape(slab_rows, seg_w)).astype(BF16)
            size = GROUP * CAP
            for s in range(segs):
                x_v[g * size : (g + 1) * size, low + s * seg_w : low + (s + 1) * seg_w] = packed[
                    s * size : (s + 1) * size
                ]
        gate_copy(p).wait()
        up_copy(p).wait()

        def gate_up(j, carry, p=p, at=at):
            cols = pl.ds(pl.multiple_of(j * hid_tile, hid_tile), hid_tile)
            gate_act = dot(x_v[:, at], gate_v[at, cols])
            up_act = dot(x_v[:, at], up_v[at, cols])
            if p < len(pieces) - 1:
                gate_act = gate_act + gate_sum[:, cols]
                up_act = up_act + up_sum[:, cols]
            if p > 0:
                gate_sum[:, cols] = gate_act
                up_sum[:, cols] = up_act
            else:
                silu = gate_act / (1.0 + jnp.exp(-gate_act))
                hidden_v[:, cols] = (silu * up_act).astype(BF16)
            return carry

        lax.fori_loop(0, hid_dev // hid_tile, gate_up, 0, unroll=2 if hid_dev > hid_tile else 1)

    others(lambda d: mass_copy(d, d).wait_recv())
    load_v[...] = jnp.sum(mass_v[...], axis=0)
    load_out = pltpu.make_async_copy(load_v, load_hbm, out_sem.at[1])
    load_out.start()

    def back_copy(p, d, src):
        at = pl.ds(pieces[p][1], pieces[p][3])
        return pltpu.make_async_remote_copy(
            src_ref=back_v.at[d, :, at], dst_ref=returned_hbm.at[src, :, at],
            send_sem=back_send_sem.at[p, d], recv_sem=back_recv_sem.at[p, src],
            device_id={"exp": d}, device_id_type=MESH,
        )

    def own_copy(p):
        at = pl.ds(pieces[p][1], pieces[p][3])
        return pltpu.make_async_copy(
            back_v.at[me, :, at], returned_hbm.at[me, :, at], own_sem.at[p]
        )

    for p, piece in forward:
        low, _, segs, seg_w = piece
        down_copy(p).wait()
        tile = min(TILE, segs * seg_w)
        for first in range(low, low + segs * seg_w, tile):
            cols = slice(first, first + tile)
            x_v[:, cols] = dot(hidden_v[...], down_v[:, cols]).astype(BF16)
        for g in range(groups):
            rows = x_v[g * GROUP * CAP : (g + 1) * GROUP * CAP, low : low + segs * seg_w]
            back_v[g * GROUP : (g + 1) * GROUP, :, slab_lanes(piece)] = pack(rows, piece)
        others(lambda d, p=p: back_copy(p, d, me).start())
        own_copy(p).start()

    mixing_out.wait()
    load_out.wait()
    others(lambda d: mass_copy(d, d).wait_send())
    for p, _ in forward:
        others(lambda d, p=p: token_copy(p, d, d).wait_send())
        others(lambda d, p=p: back_copy(p, d, d).wait_send())
        own_copy(p).wait()
    for p, _ in forward:
        others(lambda d, p=p: back_copy(p, d, d).wait_recv())


def mixing_lanes(n):
    return -(-n * CAP // 128) * 128


def combine(pieces, returned_ref, mixing_ref, load_in, out_ref, load_out):
    tok_rows = out_ref.shape[0]
    groups, _, depth = mixing_ref.shape
    for low, lane, segs, seg_w in pieces:
        mixed = jnp.zeros((segs * tok_rows, seg_w), F32)
        for g in range(groups):
            slabs = returned_ref[g * GROUP : (g + 1) * GROUP, :, lane : lane + seg_w]
            slabs = slabs.reshape(depth // 2, seg_w)
            mixing = mixing_ref[g, : segs * tok_rows, :]
            mixed = mixed + dot(mixing, jnp.concatenate([slabs, slabs], axis=0))
        for s in range(segs):
            out_ref[:, low + s * seg_w : low + (s + 1) * seg_w] = mixed[
                s * tok_rows : (s + 1) * tok_rows
            ].astype(BF16)
    load_out[...] = load_in[...].reshape(EXPERTS_ALL)


def shards(tokens, expert_ids, gate_scores, gate_weight, up_weight, down_weight):
    n = lax.axis_size("exp")
    tok_rows, width = tokens.shape
    hid_dev = gate_weight.shape[1]
    spread = FF // hid_dev
    pieces = cut(width)
    count = len(pieces)
    slab_w = pieces[-1][1] + pieces[-1][3]
    groups = n // GROUP
    cfg = (n, spread, pieces)
    dma = pltpu.SemaphoreType.DMA
    slabs = (n, SLAB, slab_w)
    mixing = (groups, SEGS * tok_rows, 2 * GROUP * SLAB)
    scratch = [
        pltpu.VMEM(tokens.shape, BF16),
        pltpu.VMEM(expert_ids.shape[::-1], jnp.int32),
        pltpu.VMEM(gate_scores.shape[::-1], F32),
        pltpu.VMEM(gate_weight.shape, BF16),
        pltpu.VMEM(up_weight.shape, BF16),
        pltpu.VMEM(down_weight.shape, BF16),
        pltpu.VMEM(slabs, BF16),
        pltpu.VMEM(slabs, BF16),
        pltpu.VMEM(slabs, BF16),
        pltpu.VMEM((n, 1, EXPERTS_ALL), F32),
        pltpu.VMEM((1, EXPERTS_ALL), F32),
        pltpu.VMEM(mixing, BF16),
        pltpu.VMEM((n * CAP, width), BF16),
        pltpu.VMEM((n * CAP, hid_dev), F32),
        pltpu.VMEM((n * CAP, hid_dev), F32),
        pltpu.VMEM((n * CAP, hid_dev), BF16),
        dma((3,)),
        dma((count,)),
        dma((count,)),
        dma((count,)),
        dma((2,)),
        dma((count,)),
        dma((count, n)),
        dma((count, n)),
        dma((n,)),
        dma((n,)),
        dma((count, n)),
        dma((count, n)),
    ]
    vmem = pl.BlockSpec(memory_space=pltpu.VMEM)
    hbm = pl.BlockSpec(memory_space=pltpu.HBM)
    partials = pl.pallas_call(
        functools.partial(kernel, cfg),
        out_shape=(
            jax.ShapeDtypeStruct(slabs, BF16),
            jax.ShapeDtypeStruct(mixing, BF16),
            jax.ShapeDtypeStruct((1, EXPERTS_ALL), F32),
        ),
        in_specs=[hbm] * 6,
        out_specs=(hbm, hbm, hbm),
        scratch_shapes=scratch,
        compiler_params=pltpu.CompilerParams(
            collective_id=0, has_side_effects=True, vmem_limit_bytes=62 * 1024 * 1024
        ),
    )(tokens, expert_ids.T, gate_scores.T, gate_weight, up_weight, down_weight)
    return pl.pallas_call(
        functools.partial(combine, pieces),
        out_shape=(
            jax.ShapeDtypeStruct(tokens.shape, BF16),
            jax.ShapeDtypeStruct((EXPERTS_ALL,), F32),
        ),
        in_specs=[vmem] * 3,
        out_specs=(vmem, vmem),
    )(*partials)


def solution(mesh):
    return jax.shard_map(
        shards,
        mesh=mesh,
        in_specs=(
            P(("rep", "exp"), None),
            P(("rep", "exp"), None),
            P(("rep", "exp"), None),
            P(None, "exp"),
            P(None, "exp"),
            P("exp", None),
        ),
        out_specs=(P(("rep", "exp"), None), P("rep")),
        check_vma=False,
    )
```

```python
import functools

import jax
import jax.numpy as jnp
from jax import lax
from jax.experimental import pallas as pl
from jax.experimental.pallas import tpu as pltpu
from jax.sharding import PartitionSpec as P

FF = 2048
EXPERTS_ALL = 384
CAP = 2
SLAB = 16
GROUP = 8
SEGS = SLAB // CAP
LANES = 128
TILE = 256
BLOCK = 512
MESH = pl.DeviceIdType.MESH
BF16 = jnp.bfloat16
F32 = jnp.float32


def dot(a, b):
    return jnp.dot(a, b, preferred_element_type=F32)


def iota(shape, dim):
    return lax.broadcasted_iota(jnp.int32, shape, dim)


def one_hot(mask):
    return jnp.where(mask, 1.0, 0.0).astype(BF16)


def slab_place(i):
    dev, seg, row = i // SLAB, (i % SLAB) // CAP, i % CAP
    return seg * (GROUP * CAP) + dev * CAP + row


def cut(width):
    pieces, low, lane = [], 0, 0
    seg_w = 2 * LANES if width % (2 * LANES) == 0 else LANES
    while low < width:
        segs = min(SEGS, (width - low) // seg_w)
        pieces.append((low, lane, segs, seg_w))
        low, lane = low + segs * seg_w, lane + seg_w
    return pieces


def blocks(first, size):
    return [pl.ds(low, min(BLOCK, first + size - low)) for low in range(first, first + size, BLOCK)]


def kernel(
    cfg,
    tokens_hbm, ids_hbm, scores_hbm, gate_hbm, up_hbm, down_hbm,
    returned_hbm, mixing_hbm, load_hbm,
    tokens_v, ids_v, scores_v, gate_v, up_v, down_v,
    send_v, arrived_v, back_v, mass_v, load_v, mixing_v, x_v, gate_sum, up_sum, hidden_v,
    small_sem, gate_sem, up_sem, down_sem, out_sem, own_sem,
    send_sem, recv_sem, mass_send_sem, mass_recv_sem, back_send_sem, back_recv_sem,
):
    n, spread, pieces = cfg
    groups = n // GROUP
    top, tok_rows = ids_v.shape
    lanes = mixing_lanes(n)
    me = lax.axis_index("exp")
    forward = list(enumerate(pieces))
    backward = forward[::-1]

    small = [
        pltpu.make_async_copy(ids_hbm, ids_v, small_sem.at[0]),
        pltpu.make_async_copy(scores_hbm, scores_v, small_sem.at[1]),
        pltpu.make_async_copy(tokens_hbm, tokens_v, small_sem.at[2]),
    ]
    for copy in small:
        copy.start()

    def columns(piece):
        low, _, segs, seg_w = piece
        return pl.ds(low, segs * seg_w)

    def gate_up_copies(p):
        low, _, segs, seg_w = pieces[p]
        copies = []
        for i, rows in enumerate(blocks(low, segs * seg_w)):
            copies += [
                pltpu.make_async_copy(gate_hbm.at[rows, :], gate_v.at[rows, :], gate_sem.at[p, i]),
                pltpu.make_async_copy(up_hbm.at[rows, :], up_v.at[rows, :], up_sem.at[p, i]),
            ]
        return copies

    def down_copies(p):
        cols = columns(pieces[p])
        return [
            pltpu.make_async_copy(down_hbm.at[rows, cols], down_v.at[rows, cols], down_sem.at[p, i])
            for i, rows in enumerate(blocks(0, down_hbm.shape[0]))
        ]

    for p, _ in backward:
        for copy in gate_up_copies(p):
            copy.start(priority=1)
    for p, _ in forward:
        for copy in down_copies(p):
            copy.start(priority=1)

    def others(body):
        def step(i, carry):
            body(lax.rem(me + i, n))
            return carry

        lax.fori_loop(1, n, step, 0, unroll=n <= 16)

    barrier = pltpu.get_barrier_semaphore()
    others(lambda d: pl.semaphore_signal(barrier, inc=1, device_id={"exp": d}, device_id_type=MESH))

    for copy in small[:2]:
        copy.wait()
    ids = jnp.transpose(ids_v[...])
    scores = jnp.transpose(scores_v[...])
    all_ids = iota((tok_rows, EXPERTS_ALL), 1)
    slot = iota((tok_rows, lanes), 1)
    slot_expert = jnp.where(slot < n * CAP, slot // (CAP * spread), -1)
    mass = jnp.zeros((tok_rows, EXPERTS_ALL), F32)
    gates = jnp.zeros((tok_rows, lanes), F32)
    hits = jnp.zeros((tok_rows, lanes), F32)
    for k in range(top):
        id_k, score_k = ids[:, k : k + 1], scores[:, k : k + 1]
        mass = mass + jnp.where(id_k == all_ids, score_k, 0.0)
        found = id_k == slot_expert
        gates = gates + jnp.where(found, score_k, 0.0)
        hits = hits + jnp.where(found, 1.0, 0.0)
    earlier = one_hot(iota((tok_rows, tok_rows), 1) < iota((tok_rows, tok_rows), 0))
    position = dot(earlier, hits.astype(BF16))
    placed = (hits > 0.5) & (position == (slot % CAP).astype(F32))
    picker = jnp.transpose(jnp.where(placed, 1.0, 0.0)).astype(BF16)
    mass_v[me] = jnp.sum(mass, axis=0, keepdims=True)

    slab_rows = GROUP * SLAB
    square = (slab_rows, slab_rows)
    to_slab = one_hot(slab_place(iota(square, 0)) == iota(square, 1))
    from_slab = one_hot(slab_place(iota(square, 1)) == iota(square, 0))

    def pack(rows, piece):
        _, _, segs, seg_w = piece
        parts = [rows[:, s * seg_w : (s + 1) * seg_w] for s in range(segs)]
        parts += [jnp.zeros_like(parts[0])] * (SEGS - segs)
        packed = jnp.concatenate(parts, axis=0)
        return dot(to_slab, packed).astype(BF16).reshape(GROUP, SLAB, seg_w)

    def slab_lanes(piece):
        return slice(piece[1], piece[1] + piece[3])

    small[2].wait()
    tokens = tokens_v[...]
    for g in range(groups):
        rows = picker[g * GROUP * CAP : (g + 1) * GROUP * CAP]
        picked = dot(rows, tokens).astype(BF16)
        for p, piece in backward:
            low, _, segs, seg_w = piece
            send_v[g * GROUP : (g + 1) * GROUP, :, slab_lanes(piece)] = pack(
                picked[:, low : low + segs * seg_w], piece
            )

    def token_copy(p, d, src):
        at = pl.ds(pieces[p][1], pieces[p][3])
        return pltpu.make_async_remote_copy(
            src_ref=send_v.at[d, :, at], dst_ref=arrived_v.at[src, :, at],
            send_sem=send_sem.at[p, d], recv_sem=recv_sem.at[p, src],
            device_id={"exp": d}, device_id_type=MESH,
        )

    def mass_copy(d, src):
        return pltpu.make_async_remote_copy(
            src_ref=mass_v.at[me], dst_ref=mass_v.at[src],
            send_sem=mass_send_sem.at[d], recv_sem=mass_recv_sem.at[src],
            device_id={"exp": d}, device_id_type=MESH,
        )

    pl.semaphore_wait(barrier, n - 1)
    for p, _ in backward:
        others(lambda d, p=p: token_copy(p, d, me).start())
    arrived_v[me] = send_v[me]
    others(lambda d: mass_copy(d, me).start())

    weights = jnp.where(placed, gates, 0.0)
    weights_hi = weights.astype(BF16)
    weights_lo = (weights - weights_hi.astype(F32)).astype(BF16)
    slab_lane = iota((lanes, slab_rows), 1)
    lane_seg = (iota((tok_rows, slab_rows), 1) % SLAB) // CAP
    for g in range(groups):
        slot_of = g * GROUP * CAP + slab_lane // SLAB * CAP + slab_lane % CAP
        spreading = one_hot(iota((lanes, slab_rows), 0) == slot_of)
        for part, term in enumerate((weights_hi, weights_lo)):
            wide = dot(term, spreading)
            for s in range(SEGS):
                mixing_v[
                    g, s * tok_rows : (s + 1) * tok_rows, part * slab_rows : (part + 1) * slab_rows
                ] = jnp.where(lane_seg == s, wide, 0.0).astype(BF16)

    mixing_out = pltpu.make_async_copy(mixing_v, mixing_hbm, out_sem.at[0])
    mixing_out.start()

    hid_dev = hidden_v.shape[1]
    hid_tile = min(TILE, hid_dev)
    for p, piece in backward:
        low, _, segs, seg_w = piece
        at = slice(low, low + segs * seg_w)
        others(lambda d, p=p: token_copy(p, d, d).wait_recv())
        for g in range(groups):
            slabs = arrived_v[g * GROUP : (g + 1) * GROUP, :, slab_lanes(piece)]
            packed = dot(from_slab, slabs.reshape(slab_rows, seg_w)).astype(BF16)
            size = GROUP * CAP
            for s in range(segs):
                x_v[g * size : (g + 1) * size, low + s * seg_w : low + (s + 1) * seg_w] = packed[
                    s * size : (s + 1) * size
                ]
        for copy in gate_up_copies(p):
            copy.wait()

        def gate_up(j, carry, p=p, at=at):
            cols = pl.ds(pl.multiple_of(j * hid_tile, hid_tile), hid_tile)
            gate_act = dot(x_v[:, at], gate_v[at, cols])
            up_act = dot(x_v[:, at], up_v[at, cols])
            if p < len(pieces) - 1:
                gate_act = gate_act + gate_sum[:, cols]
                up_act = up_act + up_sum[:, cols]
            if p > 0:
                gate_sum[:, cols] = gate_act
                up_sum[:, cols] = up_act
            else:
                silu = gate_act / (1.0 + jnp.exp(-gate_act))
                hidden_v[:, cols] = (silu * up_act).astype(BF16)
            return carry

        lax.fori_loop(0, hid_dev // hid_tile, gate_up, 0, unroll=2 if hid_dev > hid_tile else 1)

    others(lambda d: mass_copy(d, d).wait_recv())
    load_v[...] = jnp.sum(mass_v[...], axis=0)
    load_out = pltpu.make_async_copy(load_v, load_hbm, out_sem.at[1])
    load_out.start()

    def back_copy(p, d, src):
        at = pl.ds(pieces[p][1], pieces[p][3])
        return pltpu.make_async_remote_copy(
            src_ref=back_v.at[d, :, at], dst_ref=returned_hbm.at[src, :, at],
            send_sem=back_send_sem.at[p, d], recv_sem=back_recv_sem.at[p, src],
            device_id={"exp": d}, device_id_type=MESH,
        )

    def own_copy(p):
        at = pl.ds(pieces[p][1], pieces[p][3])
        return pltpu.make_async_copy(
            back_v.at[me, :, at], returned_hbm.at[me, :, at], own_sem.at[p]
        )

    for p, piece in forward:
        low, _, segs, seg_w = piece
        for copy in down_copies(p):
            copy.wait()
        tile = min(TILE, segs * seg_w)
        for first in range(low, low + segs * seg_w, tile):
            cols = slice(first, first + tile)
            x_v[:, cols] = dot(hidden_v[...], down_v[:, cols]).astype(BF16)
        for g in range(groups):
            rows = x_v[g * GROUP * CAP : (g + 1) * GROUP * CAP, low : low + segs * seg_w]
            back_v[g * GROUP : (g + 1) * GROUP, :, slab_lanes(piece)] = pack(rows, piece)
        others(lambda d, p=p: back_copy(p, d, me).start())
        own_copy(p).start()

    mixing_out.wait()
    load_out.wait()
    others(lambda d: mass_copy(d, d).wait_send())
    for p, _ in forward:
        others(lambda d, p=p: token_copy(p, d, d).wait_send())
        others(lambda d, p=p: back_copy(p, d, d).wait_send())
        own_copy(p).wait()
    for p, _ in forward:
        others(lambda d, p=p: back_copy(p, d, d).wait_recv())


def mixing_lanes(n):
    return -(-n * CAP // 128) * 128


def combine(pieces, returned_ref, mixing_ref, load_in, out_ref, load_out):
    tok_rows = out_ref.shape[0]
    groups, _, depth = mixing_ref.shape
    for low, lane, segs, seg_w in pieces:
        mixed = jnp.zeros((segs * tok_rows, seg_w), F32)
        for g in range(groups):
            slabs = returned_ref[g * GROUP : (g + 1) * GROUP, :, lane : lane + seg_w]
            slabs = slabs.reshape(depth // 2, seg_w)
            mixing = mixing_ref[g, : segs * tok_rows, :]
            mixed = mixed + dot(mixing, jnp.concatenate([slabs, slabs], axis=0))
        for s in range(segs):
            out_ref[:, low + s * seg_w : low + (s + 1) * seg_w] = mixed[
                s * tok_rows : (s + 1) * tok_rows
            ].astype(BF16)
    load_out[...] = load_in[...].reshape(EXPERTS_ALL)


def shards(tokens, expert_ids, gate_scores, gate_weight, up_weight, down_weight):
    n = lax.axis_size("exp")
    tok_rows, width = tokens.shape
    hid_dev = gate_weight.shape[1]
    spread = FF // hid_dev
    pieces = cut(width)
    count = len(pieces)
    slab_w = pieces[-1][1] + pieces[-1][3]
    groups = n // GROUP
    cfg = (n, spread, pieces)
    dma = pltpu.SemaphoreType.DMA
    slabs = (n, SLAB, slab_w)
    mixing = (groups, SEGS * tok_rows, 2 * GROUP * SLAB)
    scratch = [
        pltpu.VMEM(tokens.shape, BF16),
        pltpu.VMEM(expert_ids.shape[::-1], jnp.int32),
        pltpu.VMEM(gate_scores.shape[::-1], F32),
        pltpu.VMEM(gate_weight.shape, BF16),
        pltpu.VMEM(up_weight.shape, BF16),
        pltpu.VMEM(down_weight.shape, BF16),
        pltpu.VMEM(slabs, BF16),
        pltpu.VMEM(slabs, BF16),
        pltpu.VMEM(slabs, BF16),
        pltpu.VMEM((n, 1, EXPERTS_ALL), F32),
        pltpu.VMEM((1, EXPERTS_ALL), F32),
        pltpu.VMEM(mixing, BF16),
        pltpu.VMEM((n * CAP, width), BF16),
        pltpu.VMEM((n * CAP, hid_dev), F32),
        pltpu.VMEM((n * CAP, hid_dev), F32),
        pltpu.VMEM((n * CAP, hid_dev), BF16),
        dma((3,)),
        dma((count, -(-width // BLOCK))),
        dma((count, -(-width // BLOCK))),
        dma((count, -(-hid_dev // BLOCK))),
        dma((2,)),
        dma((count,)),
        dma((count, n)),
        dma((count, n)),
        dma((n,)),
        dma((n,)),
        dma((count, n)),
        dma((count, n)),
    ]
    vmem = pl.BlockSpec(memory_space=pltpu.VMEM)
    hbm = pl.BlockSpec(memory_space=pltpu.HBM)
    partials = pl.pallas_call(
        functools.partial(kernel, cfg),
        out_shape=(
            jax.ShapeDtypeStruct(slabs, BF16),
            jax.ShapeDtypeStruct(mixing, BF16),
            jax.ShapeDtypeStruct((1, EXPERTS_ALL), F32),
        ),
        in_specs=[hbm] * 6,
        out_specs=(hbm, hbm, hbm),
        scratch_shapes=scratch,
        compiler_params=pltpu.CompilerParams(
            collective_id=0, has_side_effects=True, vmem_limit_bytes=62 * 1024 * 1024
        ),
    )(tokens, expert_ids.T, gate_scores.T, gate_weight, up_weight, down_weight)
    return pl.pallas_call(
        functools.partial(combine, pieces),
        out_shape=(
            jax.ShapeDtypeStruct(tokens.shape, BF16),
            jax.ShapeDtypeStruct((EXPERTS_ALL,), F32),
        ),
        in_specs=[vmem] * 3,
        out_specs=(vmem, vmem),
    )(*partials)


def solution(mesh):
    return jax.shard_map(
        shards,
        mesh=mesh,
        in_specs=(
            P(("rep", "exp"), None),
            P(("rep", "exp"), None),
            P(("rep", "exp"), None),
            P(None, "exp"),
            P(None, "exp"),
            P("exp", None),
        ),
        out_specs=(P(("rep", "exp"), None), P("rep")),
        check_vma=False,
    )
```

```python
import functools

import jax
import jax.numpy as jnp
from jax import lax
from jax.experimental import pallas as pl
from jax.experimental.pallas import tpu as pltpu
from jax.sharding import PartitionSpec as P

FF = 2048
EXPERTS_ALL = 384
CAP = 2
SLAB = 16
GROUP = 8
SEGS = SLAB // CAP
LANES = 128
TILE = 512
BLOCK = 512
MESH = pl.DeviceIdType.MESH
BF16 = jnp.bfloat16
F32 = jnp.float32


def dot(a, b):
    return jnp.dot(a, b, preferred_element_type=F32)


def iota(shape, dim):
    return lax.broadcasted_iota(jnp.int32, shape, dim)


def one_hot(mask):
    return jnp.where(mask, 1.0, 0.0).astype(BF16)


def slab_place(i):
    dev, seg, row = i // SLAB, (i % SLAB) // CAP, i % CAP
    return seg * (GROUP * CAP) + dev * CAP + row


def cut(width):
    pieces, low, lane = [], 0, 0
    seg_w = 2 * LANES if width % (2 * LANES) == 0 else LANES
    while low < width:
        segs = min(SEGS, (width - low) // seg_w)
        pieces.append((low, lane, segs, seg_w))
        low, lane = low + segs * seg_w, lane + seg_w
    return pieces


def blocks(first, size):
    return [pl.ds(low, min(BLOCK, first + size - low)) for low in range(first, first + size, BLOCK)]


def kernel(
    cfg,
    tokens_hbm, ids_hbm, scores_hbm, gate_hbm, up_hbm, down_hbm,
    returned_hbm, mixing_hbm, load_hbm,
    tokens_v, ids_v, scores_v, gate_v, up_v, down_v,
    send_v, arrived_v, back_v, mass_v, load_v, mixing_v, x_v, gate_sum, up_sum, hidden_v,
    small_sem, gate_sem, up_sem, down_sem, out_sem, own_sem,
    send_sem, recv_sem, mass_send_sem, mass_recv_sem, back_send_sem, back_recv_sem,
):
    n, spread, pieces = cfg
    groups = n // GROUP
    top, tok_rows = ids_v.shape
    me = lax.axis_index("exp")
    forward = list(enumerate(pieces))
    backward = forward[::-1]

    small = [
        pltpu.make_async_copy(ids_hbm, ids_v, small_sem.at[0]),
        pltpu.make_async_copy(scores_hbm, scores_v, small_sem.at[1]),
        pltpu.make_async_copy(tokens_hbm, tokens_v, small_sem.at[2]),
    ]
    for copy in small:
        copy.start()

    def columns(piece):
        low, _, segs, seg_w = piece
        return pl.ds(low, segs * seg_w)

    def gate_up_copies(p):
        low, _, segs, seg_w = pieces[p]
        copies = []
        for i, rows in enumerate(blocks(low, segs * seg_w)):
            copies += [
                pltpu.make_async_copy(gate_hbm.at[rows, :], gate_v.at[rows, :], gate_sem.at[p, i]),
                pltpu.make_async_copy(up_hbm.at[rows, :], up_v.at[rows, :], up_sem.at[p, i]),
            ]
        return copies

    def down_copies(p):
        cols = columns(pieces[p])
        return [
            pltpu.make_async_copy(down_hbm.at[rows, cols], down_v.at[rows, cols], down_sem.at[p, i])
            for i, rows in enumerate(blocks(0, down_hbm.shape[0]))
        ]

    for p, _ in backward:
        for copy in gate_up_copies(p):
            copy.start(priority=1)
    for p, _ in forward:
        for copy in down_copies(p):
            copy.start(priority=1)

    def others(body):
        def step(i, carry):
            body(lax.rem(me + i, n))
            return carry

        lax.fori_loop(1, n, step, 0, unroll=n <= 16)

    barrier = pltpu.get_barrier_semaphore()
    others(lambda d: pl.semaphore_signal(barrier, inc=1, device_id={"exp": d}, device_id_type=MESH))

    small[0].wait()
    slots = (n * CAP, tok_rows)
    slot_expert = iota(slots, 0) // (CAP * spread)
    hits = jnp.zeros(slots, F32)
    for k in range(top):
        hits = hits + jnp.where(ids_v[k : k + 1, :] == slot_expert, 1.0, 0.0)
    earlier = one_hot(iota((tok_rows, tok_rows), 0) < iota((tok_rows, tok_rows), 1))
    position = dot(hits.astype(BF16), earlier)
    placed = (hits > 0.5) & (position == (iota(slots, 0) % CAP).astype(F32))
    picker = one_hot(placed)

    slab_rows = GROUP * SLAB
    square = (slab_rows, slab_rows)
    to_slab = one_hot(slab_place(iota(square, 0)) == iota(square, 1))
    from_slab = one_hot(slab_place(iota(square, 1)) == iota(square, 0))

    def pack(rows, piece):
        _, _, segs, seg_w = piece
        parts = [rows[:, s * seg_w : (s + 1) * seg_w] for s in range(segs)]
        parts += [jnp.zeros_like(parts[0])] * (SEGS - segs)
        packed = jnp.concatenate(parts, axis=0)
        return dot(to_slab, packed).astype(BF16).reshape(GROUP, SLAB, seg_w)

    def slab_lanes(piece):
        return slice(piece[1], piece[1] + piece[3])

    small[2].wait()
    tokens = tokens_v[...]
    for g in range(groups):
        rows = picker[g * GROUP * CAP : (g + 1) * GROUP * CAP]
        picked = dot(rows, tokens).astype(BF16)
        for p, piece in backward:
            low, _, segs, seg_w = piece
            send_v[g * GROUP : (g + 1) * GROUP, :, slab_lanes(piece)] = pack(
                picked[:, low : low + segs * seg_w], piece
            )

    def token_copy(p, d, src):
        at = pl.ds(pieces[p][1], pieces[p][3])
        return pltpu.make_async_remote_copy(
            src_ref=send_v.at[d, :, at], dst_ref=arrived_v.at[src, :, at],
            send_sem=send_sem.at[p, d], recv_sem=recv_sem.at[p, src],
            device_id={"exp": d}, device_id_type=MESH,
        )

    def mass_copy(d, src):
        return pltpu.make_async_remote_copy(
            src_ref=mass_v.at[me], dst_ref=mass_v.at[src],
            send_sem=mass_send_sem.at[d], recv_sem=mass_recv_sem.at[src],
            device_id={"exp": d}, device_id_type=MESH,
        )

    pl.semaphore_wait(barrier, n - 1)
    for p, _ in backward:
        others(lambda d, p=p: token_copy(p, d, me).start())
    arrived_v[me] = send_v[me]

    small[1].wait()
    ids = jnp.transpose(ids_v[...])
    scores = jnp.transpose(scores_v[...])
    all_ids = iota((tok_rows, EXPERTS_ALL), 1)
    mass = jnp.zeros((tok_rows, EXPERTS_ALL), F32)
    for k in range(top):
        mass = mass + jnp.where(ids[:, k : k + 1] == all_ids, scores[:, k : k + 1], 0.0)
    mass_v[me] = jnp.sum(mass, axis=0, keepdims=True)
    others(lambda d: mass_copy(d, me).start())

    gates = jnp.zeros(slots, F32)
    for k in range(top):
        found = ids_v[k : k + 1, :] == slot_expert
        gates = gates + jnp.where(found, scores_v[k : k + 1, :], 0.0)
    weights = jnp.where(placed, gates, 0.0)
    weights_hi = weights.astype(BF16)
    weights_lo = (weights - weights_hi.astype(F32)).astype(BF16)
    slab_lane = iota((n * CAP, slab_rows), 1)
    lane_seg = (iota((tok_rows, slab_rows), 1) % SLAB) // CAP
    for g in range(groups):
        slot_of = g * GROUP * CAP + slab_lane // SLAB * CAP + slab_lane % CAP
        spreading = one_hot(iota((n * CAP, slab_rows), 0) == slot_of)
        for part, term in enumerate((weights_hi, weights_lo)):
            wide = lax.dot_general(
                term, spreading, (((0,), (0,)), ((), ())), preferred_element_type=F32
            )
            for s in range(SEGS):
                mixing_v[
                    g, s * tok_rows : (s + 1) * tok_rows, part * slab_rows : (part + 1) * slab_rows
                ] = jnp.where(lane_seg == s, wide, 0.0).astype(BF16)
    mixing_out = pltpu.make_async_copy(mixing_v, mixing_hbm, out_sem.at[0])
    mixing_out.start()

    hid_dev = hidden_v.shape[1]
    hid_tile = min(TILE, hid_dev)
    for p, piece in backward:
        low, _, segs, seg_w = piece
        at = slice(low, low + segs * seg_w)
        others(lambda d, p=p: token_copy(p, d, d).wait_recv())
        for g in range(groups):
            slabs = arrived_v[g * GROUP : (g + 1) * GROUP, :, slab_lanes(piece)]
            packed = dot(from_slab, slabs.reshape(slab_rows, seg_w)).astype(BF16)
            size = GROUP * CAP
            for s in range(segs):
                x_v[g * size : (g + 1) * size, low + s * seg_w : low + (s + 1) * seg_w] = packed[
                    s * size : (s + 1) * size
                ]
        for copy in gate_up_copies(p):
            copy.wait()

        def gate_up(j, carry, p=p, at=at):
            cols = pl.ds(pl.multiple_of(j * hid_tile, hid_tile), hid_tile)
            gate_act = dot(x_v[:, at], gate_v[at, cols])
            up_act = dot(x_v[:, at], up_v[at, cols])
            if p < len(pieces) - 1:
                gate_act = gate_act + gate_sum[:, cols]
                up_act = up_act + up_sum[:, cols]
            if p > 0:
                gate_sum[:, cols] = gate_act
                up_sum[:, cols] = up_act
            else:
                silu = gate_act / (1.0 + jnp.exp(-gate_act))
                hidden_v[:, cols] = (silu * up_act).astype(BF16)
            return carry

        lax.fori_loop(0, hid_dev // hid_tile, gate_up, 0)

    others(lambda d: mass_copy(d, d).wait_recv())
    load_v[...] = jnp.sum(mass_v[...], axis=0)
    load_out = pltpu.make_async_copy(load_v, load_hbm, out_sem.at[1])
    load_out.start()

    def back_copy(p, d, src):
        at = pl.ds(pieces[p][1], pieces[p][3])
        return pltpu.make_async_remote_copy(
            src_ref=back_v.at[d, :, at], dst_ref=returned_hbm.at[src, :, at],
            send_sem=back_send_sem.at[p, d], recv_sem=back_recv_sem.at[p, src],
            device_id={"exp": d}, device_id_type=MESH,
        )

    def own_copy(p):
        at = pl.ds(pieces[p][1], pieces[p][3])
        return pltpu.make_async_copy(
            back_v.at[me, :, at], returned_hbm.at[me, :, at], own_sem.at[p]
        )

    for p, piece in forward:
        low, _, segs, seg_w = piece
        for copy in down_copies(p):
            copy.wait()
        tile = min(TILE, segs * seg_w)
        for first in range(low, low + segs * seg_w, tile):
            cols = slice(first, first + tile)
            x_v[:, cols] = dot(hidden_v[...], down_v[:, cols]).astype(BF16)
        for g in range(groups):
            rows = x_v[g * GROUP * CAP : (g + 1) * GROUP * CAP, low : low + segs * seg_w]
            back_v[g * GROUP : (g + 1) * GROUP, :, slab_lanes(piece)] = pack(rows, piece)
        others(lambda d, p=p: back_copy(p, d, me).start())
        own_copy(p).start()

    mixing_out.wait()
    load_out.wait()
    others(lambda d: mass_copy(d, d).wait_send())
    for p, _ in forward:
        others(lambda d, p=p: token_copy(p, d, d).wait_send())
        others(lambda d, p=p: back_copy(p, d, d).wait_send())
        own_copy(p).wait()
    for p, _ in forward:
        others(lambda d, p=p: back_copy(p, d, d).wait_recv())


def combine(pieces, returned_ref, mixing_ref, load_in, out_ref, load_out):
    tok_rows = out_ref.shape[0]
    groups, _, depth = mixing_ref.shape
    for low, lane, segs, seg_w in pieces:
        mixed = jnp.zeros((segs * tok_rows, seg_w), F32)
        for g in range(groups):
            slabs = returned_ref[g * GROUP : (g + 1) * GROUP, :, lane : lane + seg_w]
            slabs = slabs.reshape(depth // 2, seg_w)
            mixing = mixing_ref[g, : segs * tok_rows, :]
            mixed = mixed + dot(mixing, jnp.concatenate([slabs, slabs], axis=0))
        for s in range(segs):
            out_ref[:, low + s * seg_w : low + (s + 1) * seg_w] = mixed[
                s * tok_rows : (s + 1) * tok_rows
            ].astype(BF16)
    load_out[...] = load_in[...].reshape(EXPERTS_ALL)


def shards(tokens, expert_ids, gate_scores, gate_weight, up_weight, down_weight):
    n = lax.axis_size("exp")
    tok_rows, width = tokens.shape
    hid_dev = gate_weight.shape[1]
    spread = FF // hid_dev
    pieces = cut(width)
    count = len(pieces)
    slab_w = pieces[-1][1] + pieces[-1][3]
    groups = n // GROUP
    cfg = (n, spread, pieces)
    dma = pltpu.SemaphoreType.DMA
    slabs = (n, SLAB, slab_w)
    mixing = (groups, SEGS * tok_rows, 2 * GROUP * SLAB)
    scratch = [
        pltpu.VMEM(tokens.shape, BF16),
        pltpu.VMEM(expert_ids.shape[::-1], jnp.int32),
        pltpu.VMEM(gate_scores.shape[::-1], F32),
        pltpu.VMEM(gate_weight.shape, BF16),
        pltpu.VMEM(up_weight.shape, BF16),
        pltpu.VMEM(down_weight.shape, BF16),
        pltpu.VMEM(slabs, BF16),
        pltpu.VMEM(slabs, BF16),
        pltpu.VMEM(slabs, BF16),
        pltpu.VMEM((n, 1, EXPERTS_ALL), F32),
        pltpu.VMEM((1, EXPERTS_ALL), F32),
        pltpu.VMEM(mixing, BF16),
        pltpu.VMEM((n * CAP, width), BF16),
        pltpu.VMEM((n * CAP, hid_dev), F32),
        pltpu.VMEM((n * CAP, hid_dev), F32),
        pltpu.VMEM((n * CAP, hid_dev), BF16),
        dma((3,)),
        dma((count, -(-width // BLOCK))),
        dma((count, -(-width // BLOCK))),
        dma((count, -(-hid_dev // BLOCK))),
        dma((2,)),
        dma((count,)),
        dma((count, n)),
        dma((count, n)),
        dma((n,)),
        dma((n,)),
        dma((count, n)),
        dma((count, n)),
    ]
    vmem = pl.BlockSpec(memory_space=pltpu.VMEM)
    hbm = pl.BlockSpec(memory_space=pltpu.HBM)
    partials = pl.pallas_call(
        functools.partial(kernel, cfg),
        out_shape=(
            jax.ShapeDtypeStruct(slabs, BF16),
            jax.ShapeDtypeStruct(mixing, BF16),
            jax.ShapeDtypeStruct((1, EXPERTS_ALL), F32),
        ),
        in_specs=[hbm] * 6,
        out_specs=(hbm, hbm, hbm),
        scratch_shapes=scratch,
        compiler_params=pltpu.CompilerParams(
            collective_id=0, has_side_effects=True, vmem_limit_bytes=62 * 1024 * 1024
        ),
    )(tokens, expert_ids.T, gate_scores.T, gate_weight, up_weight, down_weight)
    return pl.pallas_call(
        functools.partial(combine, pieces),
        out_shape=(
            jax.ShapeDtypeStruct(tokens.shape, BF16),
            jax.ShapeDtypeStruct((EXPERTS_ALL,), F32),
        ),
        in_specs=[vmem] * 3,
        out_specs=(vmem, vmem),
    )(*partials)


def solution(mesh):
    return jax.shard_map(
        shards,
        mesh=mesh,
        in_specs=(
            P(("rep", "exp"), None),
            P(("rep", "exp"), None),
            P(("rep", "exp"), None),
            P(None, "exp"),
            P(None, "exp"),
            P("exp", None),
        ),
        out_specs=(P(("rep", "exp"), None), P("rep")),
        check_vma=False,
    )
```

```python
import functools

import jax
import jax.numpy as jnp
from jax import lax
from jax.experimental import pallas as pl
from jax.experimental.pallas import tpu as pltpu
from jax.sharding import PartitionSpec as P

FF = 2048
EXPERTS_ALL = 384
CAP = 2
SLAB = 16
GROUP = 8
SEGS = SLAB // CAP
LANES = 128
TILE = 512
BLOCK = 512
MESH = pl.DeviceIdType.MESH
BF16 = jnp.bfloat16
F32 = jnp.float32


def dot(a, b):
    return jnp.dot(a, b, preferred_element_type=F32)


def iota(shape, dim):
    return lax.broadcasted_iota(jnp.int32, shape, dim)


def one_hot(mask):
    return jnp.where(mask, 1.0, 0.0).astype(BF16)


def slab_place(i):
    dev, seg, row = i // SLAB, (i % SLAB) // CAP, i % CAP
    return seg * (GROUP * CAP) + dev * CAP + row


def cut(width, fine):
    pieces, low, lane = [], 0, 0
    wide = 2 * LANES if width % (2 * LANES) == 0 else LANES
    while low < width:
        seg_w = LANES if fine and width - low < wide * SEGS else wide
        segs = min(SEGS, (width - low) // seg_w)
        pieces.append((low, lane, segs, seg_w))
        low, lane = low + segs * seg_w, lane + seg_w
    return pieces


def blocks(first, size):
    return [pl.ds(low, min(BLOCK, first + size - low)) for low in range(first, first + size, BLOCK)]


def kernel(
    cfg,
    tokens_hbm, ids_hbm, scores_hbm, gate_hbm, up_hbm, down_hbm,
    out_ref, load_ref,
    tokens_v, ids_v, scores_v, gate_v, up_v, down_v,
    send_v, arrived_v, back_v, returned_v, mass_v, mixing_v, x_v, gate_sum, up_sum, hidden_v,
    small_sem, gate_sem, up_sem, down_sem,
    send_sem, recv_sem, mass_send_sem, mass_recv_sem, back_send_sem, back_recv_sem,
):
    n, spread, pieces, back_pieces = cfg
    groups = n // GROUP
    top, tok_rows = ids_v.shape
    me = lax.axis_index("exp")
    forward = list(enumerate(back_pieces))
    backward = list(enumerate(pieces))[::-1]

    small = [
        pltpu.make_async_copy(ids_hbm, ids_v, small_sem.at[0]),
        pltpu.make_async_copy(scores_hbm, scores_v, small_sem.at[1]),
        pltpu.make_async_copy(tokens_hbm, tokens_v, small_sem.at[2]),
    ]
    for copy in small:
        copy.start()

    def columns(piece):
        low, _, segs, seg_w = piece
        return pl.ds(low, segs * seg_w)

    def gate_up_copies(p):
        low, _, segs, seg_w = pieces[p]
        copies = []
        for i, rows in enumerate(blocks(low, segs * seg_w)):
            copies += [
                pltpu.make_async_copy(gate_hbm.at[rows, :], gate_v.at[rows, :], gate_sem.at[p, i]),
                pltpu.make_async_copy(up_hbm.at[rows, :], up_v.at[rows, :], up_sem.at[p, i]),
            ]
        return copies

    def down_copies(p):
        cols = columns(back_pieces[p])
        return [
            pltpu.make_async_copy(down_hbm.at[rows, cols], down_v.at[rows, cols], down_sem.at[p, i])
            for i, rows in enumerate(blocks(0, down_hbm.shape[0]))
        ]

    for copy in gate_up_copies(backward[0][0]):
        copy.start()

    def others(body):
        def step(i, carry):
            body(lax.rem(me + i, n))
            return carry

        lax.fori_loop(1, n, step, 0, unroll=n <= 16)

    barrier = pltpu.get_barrier_semaphore()
    others(lambda d: pl.semaphore_signal(barrier, inc=1, device_id={"exp": d}, device_id_type=MESH))

    small[0].wait()
    slots = (n * CAP, tok_rows)
    slot_expert = iota(slots, 0) // (CAP * spread)
    hits = jnp.zeros(slots, F32)
    for k in range(top):
        hits = hits + jnp.where(ids_v[k : k + 1, :] == slot_expert, 1.0, 0.0)
    earlier = one_hot(iota((tok_rows, tok_rows), 0) < iota((tok_rows, tok_rows), 1))
    position = dot(hits.astype(BF16), earlier)
    placed = (hits > 0.5) & (position == (iota(slots, 0) % CAP).astype(F32))
    picker = one_hot(placed)

    slab_rows = GROUP * SLAB
    square = (slab_rows, slab_rows)
    to_slab = one_hot(slab_place(iota(square, 0)) == iota(square, 1))
    from_slab = one_hot(slab_place(iota(square, 1)) == iota(square, 0))

    def pack(rows, piece):
        _, _, segs, seg_w = piece
        parts = [rows[:, s * seg_w : (s + 1) * seg_w] for s in range(segs)]
        parts += [jnp.zeros_like(parts[0])] * (SEGS - segs)
        packed = jnp.concatenate(parts, axis=0)
        return dot(to_slab, packed).astype(BF16).reshape(GROUP, SLAB, seg_w)

    def slab_lanes(piece):
        return slice(piece[1], piece[1] + piece[3])

    small[2].wait()
    tokens = tokens_v[...]
    for g in range(groups):
        rows = picker[g * GROUP * CAP : (g + 1) * GROUP * CAP]
        picked = dot(rows, tokens).astype(BF16)
        for p, piece in backward:
            low, _, segs, seg_w = piece
            send_v[g * GROUP : (g + 1) * GROUP, :, slab_lanes(piece)] = pack(
                picked[:, low : low + segs * seg_w], piece
            )

    def token_copy(p, d, src):
        at = pl.ds(pieces[p][1], pieces[p][3])
        return pltpu.make_async_remote_copy(
            src_ref=send_v.at[d, :, at], dst_ref=arrived_v.at[src, :, at],
            send_sem=send_sem.at[p, d], recv_sem=recv_sem.at[p, src],
            device_id={"exp": d}, device_id_type=MESH,
        )

    def mass_copy(d, src):
        return pltpu.make_async_remote_copy(
            src_ref=mass_v.at[me], dst_ref=mass_v.at[src],
            send_sem=mass_send_sem.at[d], recv_sem=mass_recv_sem.at[src],
            device_id={"exp": d}, device_id_type=MESH,
        )

    pl.semaphore_wait(barrier, n - 1)
    for p, _ in backward:
        others(lambda d, p=p: token_copy(p, d, me).start())
    for p, _ in backward[1:]:
        for copy in gate_up_copies(p):
            copy.start()
    for p, _ in forward:
        for copy in down_copies(p):
            copy.start()
    arrived_v[me] = send_v[me]

    small[1].wait()
    ids = jnp.transpose(ids_v[...])
    scores = jnp.transpose(scores_v[...])
    all_ids = iota((tok_rows, EXPERTS_ALL), 1)
    mass = jnp.zeros((tok_rows, EXPERTS_ALL), F32)
    for k in range(top):
        mass = mass + jnp.where(ids[:, k : k + 1] == all_ids, scores[:, k : k + 1], 0.0)
    mass_v[me] = jnp.sum(mass, axis=0, keepdims=True)
    others(lambda d: mass_copy(d, me).start())

    gates = jnp.zeros(slots, F32)
    for k in range(top):
        found = ids_v[k : k + 1, :] == slot_expert
        gates = gates + jnp.where(found, scores_v[k : k + 1, :], 0.0)
    weights = jnp.where(placed, gates, 0.0)
    weights_hi = weights.astype(BF16)
    weights_lo = (weights - weights_hi.astype(F32)).astype(BF16)
    slab_lane = iota((n * CAP, slab_rows), 1)
    lane_seg = (iota((tok_rows, slab_rows), 1) % SLAB) // CAP
    for g in range(groups):
        slot_of = g * GROUP * CAP + slab_lane // SLAB * CAP + slab_lane % CAP
        spreading = one_hot(iota((n * CAP, slab_rows), 0) == slot_of)
        for part, term in enumerate((weights_hi, weights_lo)):
            wide = lax.dot_general(
                term, spreading, (((0,), (0,)), ((), ())), preferred_element_type=F32
            )
            for s in range(SEGS):
                mixing_v[
                    g, s * tok_rows : (s + 1) * tok_rows, part * slab_rows : (part + 1) * slab_rows
                ] = jnp.where(lane_seg == s, wide, 0.0).astype(BF16)

    hid_dev = hidden_v.shape[1]
    hid_tile = min(TILE, hid_dev)
    for p, piece in backward:
        low, _, segs, seg_w = piece
        at = slice(low, low + segs * seg_w)
        others(lambda d, p=p: token_copy(p, d, d).wait_recv())
        for g in range(groups):
            slabs = arrived_v[g * GROUP : (g + 1) * GROUP, :, slab_lanes(piece)]
            packed = dot(from_slab, slabs.reshape(slab_rows, seg_w)).astype(BF16)
            size = GROUP * CAP
            for s in range(segs):
                x_v[g * size : (g + 1) * size, low + s * seg_w : low + (s + 1) * seg_w] = packed[
                    s * size : (s + 1) * size
                ]
        for copy in gate_up_copies(p):
            copy.wait()

        def gate_up(j, carry, p=p, at=at):
            cols = pl.ds(pl.multiple_of(j * hid_tile, hid_tile), hid_tile)
            gate_act = dot(x_v[:, at], gate_v[at, cols])
            up_act = dot(x_v[:, at], up_v[at, cols])
            if p < len(pieces) - 1:
                gate_act = gate_act + gate_sum[:, cols]
                up_act = up_act + up_sum[:, cols]
            if p > 0:
                gate_sum[:, cols] = gate_act
                up_sum[:, cols] = up_act
            else:
                silu = gate_act / (1.0 + jnp.exp(-gate_act))
                hidden_v[:, cols] = (silu * up_act).astype(BF16)
            return carry

        lax.fori_loop(0, hid_dev // hid_tile, gate_up, 0)

    others(lambda d: mass_copy(d, d).wait_recv())
    load_ref[...] = jnp.sum(mass_v[...], axis=0).reshape(EXPERTS_ALL)

    def back_copy(p, d, src):
        at = pl.ds(back_pieces[p][1], back_pieces[p][3])
        return pltpu.make_async_remote_copy(
            src_ref=back_v.at[d, :, at], dst_ref=returned_v.at[src, :, at],
            send_sem=back_send_sem.at[p, d], recv_sem=back_recv_sem.at[p, src],
            device_id={"exp": d}, device_id_type=MESH,
        )

    for p, piece in forward:
        low, _, segs, seg_w = piece
        for copy in down_copies(p):
            copy.wait()
        tile = min(TILE, segs * seg_w)
        for first in range(low, low + segs * seg_w, tile):
            cols = slice(first, first + tile)
            x_v[:, cols] = dot(hidden_v[...], down_v[:, cols]).astype(BF16)
        for g in range(groups):
            rows = x_v[g * GROUP * CAP : (g + 1) * GROUP * CAP, low : low + segs * seg_w]
            back_v[g * GROUP : (g + 1) * GROUP, :, slab_lanes(piece)] = pack(rows, piece)
        others(lambda d, p=p: back_copy(p, d, me).start())
        returned_v[me, :, slab_lanes(piece)] = back_v[me, :, slab_lanes(piece)]

    for p, piece in forward:
        others(lambda d, p=p: back_copy(p, d, d).wait_recv())
        combine(piece, returned_v, mixing_v, out_ref)
    others(lambda d: mass_copy(d, d).wait_send())
    for p, _ in backward:
        others(lambda d, p=p: token_copy(p, d, d).wait_send())
    for p, _ in forward:
        others(lambda d, p=p: back_copy(p, d, d).wait_send())


def combine(piece, returned_ref, mixing_ref, out_ref):
    low, lane, segs, seg_w = piece
    tok_rows = out_ref.shape[0]
    groups, _, depth = mixing_ref.shape
    mixed = jnp.zeros((segs * tok_rows, seg_w), F32)
    for g in range(groups):
        slabs = returned_ref[g * GROUP : (g + 1) * GROUP, :, lane : lane + seg_w]
        slabs = slabs.reshape(depth // 2, seg_w)
        mixing = mixing_ref[g, : segs * tok_rows, :]
        mixed = mixed + dot(mixing, jnp.concatenate([slabs, slabs], axis=0))
    for s in range(segs):
        out_ref[:, low + s * seg_w : low + (s + 1) * seg_w] = mixed[
            s * tok_rows : (s + 1) * tok_rows
        ].astype(BF16)


def copy_out(combined_in, load_in, combined_out, load_out):
    combined_out[...] = combined_in[...]
    load_out[...] = load_in[...]


def shards(tokens, expert_ids, gate_scores, gate_weight, up_weight, down_weight):
    n = lax.axis_size("exp")
    tok_rows, width = tokens.shape
    hid_dev = gate_weight.shape[1]
    spread = FF // hid_dev
    pieces, back_pieces = cut(width, False), cut(width, True)
    count, back_count = len(pieces), len(back_pieces)
    slab_w = max(lane + seg_w for _, lane, _, seg_w in pieces + back_pieces)
    groups = n // GROUP
    cfg = (n, spread, pieces, back_pieces)
    dma = pltpu.SemaphoreType.DMA
    slabs = (n, SLAB, slab_w)
    mixing = (groups, SEGS * tok_rows, 2 * GROUP * SLAB)
    scratch = [
        pltpu.VMEM(tokens.shape, BF16),
        pltpu.VMEM(expert_ids.shape[::-1], jnp.int32),
        pltpu.VMEM(gate_scores.shape[::-1], F32),
        pltpu.VMEM(gate_weight.shape, BF16),
        pltpu.VMEM(up_weight.shape, BF16),
        pltpu.VMEM(down_weight.shape, BF16),
        pltpu.VMEM(slabs, BF16),
        pltpu.VMEM(slabs, BF16),
        pltpu.VMEM(slabs, BF16),
        pltpu.VMEM(slabs, BF16),
        pltpu.VMEM((n, 1, EXPERTS_ALL), F32),
        pltpu.VMEM(mixing, BF16),
        pltpu.VMEM((n * CAP, width), BF16),
        pltpu.VMEM((n * CAP, hid_dev), F32),
        pltpu.VMEM((n * CAP, hid_dev), F32),
        pltpu.VMEM((n * CAP, hid_dev), BF16),
        dma((3,)),
        dma((count, -(-width // BLOCK))),
        dma((count, -(-width // BLOCK))),
        dma((back_count, -(-hid_dev // BLOCK))),
        dma((count, n)),
        dma((count, n)),
        dma((n,)),
        dma((n,)),
        dma((back_count, n)),
        dma((back_count, n)),
    ]
    vmem = pl.BlockSpec(memory_space=pltpu.VMEM)
    hbm = pl.BlockSpec(memory_space=pltpu.HBM)
    out_shape = (
        jax.ShapeDtypeStruct(tokens.shape, BF16),
        jax.ShapeDtypeStruct((EXPERTS_ALL,), F32),
    )
    results = pl.pallas_call(
        functools.partial(kernel, cfg),
        out_shape=out_shape,
        in_specs=[hbm] * 6,
        out_specs=(vmem, vmem),
        scratch_shapes=scratch,
        compiler_params=pltpu.CompilerParams(
            collective_id=0, has_side_effects=True, vmem_limit_bytes=62 * 1024 * 1024
        ),
    )(tokens, expert_ids.T, gate_scores.T, gate_weight, up_weight, down_weight)
    return pl.pallas_call(
        copy_out, out_shape=out_shape, in_specs=[vmem, vmem], out_specs=(vmem, vmem)
    )(*results)


def solution(mesh):
    return jax.shard_map(
        shards,
        mesh=mesh,
        in_specs=(
            P(("rep", "exp"), None),
            P(("rep", "exp"), None),
            P(("rep", "exp"), None),
            P(None, "exp"),
            P(None, "exp"),
            P("exp", None),
        ),
        out_specs=(P(("rep", "exp"), None), P("rep")),
        check_vma=False,
    )
```

```python
import functools

import jax
import jax.numpy as jnp
from jax import lax
from jax.experimental import pallas as pl
from jax.experimental.pallas import tpu as pltpu
from jax.sharding import PartitionSpec as P

FF = 2048
EXPERTS_ALL = 384
CAP = 2
SLAB = 16
GROUP = 8
TILE = 256
MESH = pl.DeviceIdType.MESH
BF16 = jnp.bfloat16
F32 = jnp.float32


def dot(a, b):
    return jnp.dot(a, b, preferred_element_type=F32)


def iota(shape, dim):
    return lax.broadcasted_iota(jnp.int32, shape, dim)


def one_hot(mask):
    return jnp.where(mask, 1.0, 0.0).astype(BF16)


def slab_place(i, segs):
    dev, seg, row = i // SLAB, (i % SLAB) // CAP, i % CAP
    return jnp.where(seg < segs, seg * (GROUP * CAP) + dev * CAP + row, -1)


def kernel(
    cfg,
    tokens_hbm, ids_hbm, scores_hbm, gate_hbm, up_hbm, down_hbm,
    out_ref, load_ref,
    tokens_v, ids_v, scores_v, gate_v, up_v, down_v,
    send_v, arrived_v, back_v, returned_v, mass_v, mixing_v, x_v, gate_sum, up_sum, hidden_v,
    small_sem, gate_sem, up_sem, down_sem,
    send_sem, recv_sem, back_send_sem, back_recv_sem,
):
    n, spread, segs, pieces, piece_w, seg_w = cfg
    groups = n // GROUP
    top, tok_rows = ids_v.shape
    me = lax.axis_index("exp")

    small = [
        pltpu.make_async_copy(ids_hbm, ids_v, small_sem.at[0]),
        pltpu.make_async_copy(scores_hbm, scores_v, small_sem.at[1]),
        pltpu.make_async_copy(tokens_hbm, tokens_v, small_sem.at[2]),
    ]
    for copy in small:
        copy.start()

    def gate_copy(p):
        return pltpu.make_async_copy(
            gate_hbm.at[pl.ds(p * piece_w, piece_w), :], gate_v.at[p], gate_sem.at[p]
        )

    def up_copy(p):
        return pltpu.make_async_copy(
            up_hbm.at[pl.ds(p * piece_w, piece_w), :], up_v.at[p], up_sem.at[p]
        )

    def down_copy(p):
        return pltpu.make_async_copy(
            down_hbm.at[:, pl.ds(p * piece_w, piece_w)], down_v.at[p], down_sem.at[p]
        )

    gate_copy(0).start()
    up_copy(0).start()

    def others(body):
        def step(i, carry):
            body(lax.rem(me + i, n))
            return carry

        lax.fori_loop(1, n, step, 0, unroll=n <= 16)

    barrier = pltpu.get_barrier_semaphore()
    others(lambda d: pl.semaphore_signal(barrier, inc=1, device_id={"exp": d}, device_id_type=MESH))

    small[0].wait()
    slots = (n * CAP, tok_rows)
    slot_expert = iota(slots, 0) // (CAP * spread)
    hits = jnp.zeros(slots, F32)
    for k in range(top):
        hits = hits + jnp.where(ids_v[k : k + 1, :] == slot_expert, 1.0, 0.0)
    earlier = one_hot(iota((tok_rows, tok_rows), 0) < iota((tok_rows, tok_rows), 1))
    position = dot(hits.astype(BF16), earlier)
    placed = (hits > 0.5) & (position == (iota(slots, 0) % CAP).astype(F32))
    picker = one_hot(placed)

    slab_rows, packed_rows = GROUP * SLAB, segs * GROUP * CAP
    to_slab = one_hot(
        slab_place(iota((slab_rows, packed_rows), 0), segs) == iota((slab_rows, packed_rows), 1)
    )
    from_slab = one_hot(
        slab_place(iota((packed_rows, slab_rows), 1), segs) == iota((packed_rows, slab_rows), 0)
    )

    def pack(rows):
        packed = jnp.concatenate([rows[:, s * seg_w : (s + 1) * seg_w] for s in range(segs)], axis=0)
        return dot(to_slab, packed)

    small[2].wait()
    tokens = tokens_v[...]
    for g in range(groups):
        rows = picker[g * GROUP * CAP : (g + 1) * GROUP * CAP]
        picked = dot(rows, tokens).astype(BF16)
        for p in range(pieces):
            slabs = pack(picked[:, p * piece_w : (p + 1) * piece_w]).astype(BF16)
            send_v[g * GROUP : (g + 1) * GROUP, :, p * seg_w : (p + 1) * seg_w] = slabs.reshape(
                GROUP, SLAB, seg_w
            )

    def token_copy(d, src):
        return pltpu.make_async_remote_copy(
            src_ref=send_v.at[d], dst_ref=arrived_v.at[src],
            send_sem=send_sem.at[d], recv_sem=recv_sem.at[src],
            device_id={"exp": d}, device_id_type=MESH,
        )

    pl.semaphore_wait(barrier, n - 1)
    others(lambda d: token_copy(d, me).start())
    for p in range(1, pieces):
        gate_copy(p).start()
        up_copy(p).start()
    for p in range(pieces):
        down_copy(p).start()
    arrived_v[me] = send_v[me]

    small[1].wait()
    ids = jnp.transpose(ids_v[...])
    scores = jnp.transpose(scores_v[...])
    mass_w = pieces * seg_w
    all_ids = iota((tok_rows, mass_w), 1)
    mass = jnp.zeros((tok_rows, mass_w), F32)
    for k in range(top):
        mass = mass + jnp.where(ids[:, k : k + 1] == all_ids, scores[:, k : k + 1], 0.0)
    mass = jnp.sum(mass, axis=0, keepdims=True)
    mass_hi = mass.astype(BF16).astype(F32)
    mass_v[0:1] = mass_hi
    mass_v[1:2] = mass - mass_hi
    slab_row = iota((slab_rows, seg_w), 0) % SLAB
    hi_row, lo_row = slab_row == SLAB - 2, slab_row == SLAB - 1

    gates = jnp.zeros(slots, F32)
    for k in range(top):
        found = ids_v[k : k + 1, :] == slot_expert
        gates = gates + jnp.where(found, scores_v[k : k + 1, :], 0.0)
    weights = jnp.where(placed, gates, 0.0)
    weights_hi = weights.astype(BF16)
    weights_lo = (weights - weights_hi.astype(F32)).astype(BF16)
    slab_lane = iota((n * CAP, slab_rows), 1)
    lane_seg = (iota((tok_rows, slab_rows), 1) % SLAB) // CAP
    for g in range(groups):
        slot_of = g * GROUP * CAP + slab_lane // SLAB * CAP + slab_lane % CAP
        spreading = one_hot(iota((n * CAP, slab_rows), 0) == slot_of)
        for part, term in enumerate((weights_hi, weights_lo)):
            wide = lax.dot_general(
                term, spreading, (((0,), (0,)), ((), ())), preferred_element_type=F32
            )
            for s in range(segs):
                mixing_v[
                    g, s * tok_rows : (s + 1) * tok_rows, part * slab_rows : (part + 1) * slab_rows
                ] = jnp.where(lane_seg == s, wide, 0.0).astype(BF16)

    hid_dev = hidden_v.shape[1]
    hid_tile = min(TILE, hid_dev)
    others(lambda d: token_copy(d, d).wait_recv())
    for p in range(pieces):
        for g in range(groups):
            slabs = arrived_v[g * GROUP : (g + 1) * GROUP, :, p * seg_w : (p + 1) * seg_w]
            packed = dot(from_slab, slabs.reshape(slab_rows, seg_w)).astype(BF16)
            size = GROUP * CAP
            for s in range(segs):
                x_v[g * size : (g + 1) * size, s * seg_w : (s + 1) * seg_w] = packed[
                    s * size : (s + 1) * size
                ]
        gate_copy(p).wait()
        up_copy(p).wait()

        def gate_up(j, carry, p=p):
            cols = pl.ds(pl.multiple_of(j * hid_tile, hid_tile), hid_tile)
            gate_act = dot(x_v[...], gate_v[p, :, cols])
            up_act = dot(x_v[...], up_v[p, :, cols])
            if p > 0:
                gate_act = gate_act + gate_sum[:, cols]
                up_act = up_act + up_sum[:, cols]
            if p < pieces - 1:
                gate_sum[:, cols] = gate_act
                up_sum[:, cols] = up_act
            else:
                silu = gate_act / (1.0 + jnp.exp(-gate_act))
                hidden_v[:, cols] = (silu * up_act).astype(BF16)
            return carry

        lax.fori_loop(0, hid_dev // hid_tile, gate_up, 0)

    def back_copy(p, d, src):
        return pltpu.make_async_remote_copy(
            src_ref=back_v.at[p, d], dst_ref=returned_v.at[p, src],
            send_sem=back_send_sem.at[p, d], recv_sem=back_recv_sem.at[p, src],
            device_id={"exp": d}, device_id_type=MESH,
        )

    for p in range(pieces):
        down_copy(p).wait()
        for s in range(segs):
            cols = slice(s * seg_w, (s + 1) * seg_w)
            x_v[:, cols] = dot(hidden_v[...], down_v[p, :, cols]).astype(BF16)
        for g in range(groups):
            rows = x_v[g * GROUP * CAP : (g + 1) * GROUP * CAP]
            at = slice(p * seg_w, (p + 1) * seg_w)
            spare = jnp.where(lo_row, mass_v[1:2, at], jnp.where(hi_row, mass_v[0:1, at], 0.0))
            slabs = (pack(rows) + spare).astype(BF16)
            back_v[p, g * GROUP : (g + 1) * GROUP] = slabs.reshape(GROUP, SLAB, seg_w)
        others(lambda d, p=p: back_copy(p, d, me).start())
        returned_v[p, me] = back_v[p, me]

    load = []
    for p in range(pieces):
        others(lambda d, p=p: back_copy(p, d, d).wait_recv())
        mixed = jnp.zeros((segs * tok_rows, seg_w), F32)
        for g in range(groups):
            slabs = returned_v[p, g * GROUP : (g + 1) * GROUP].reshape(slab_rows, seg_w)
            mixed = mixed + dot(mixing_v[g], jnp.concatenate([slabs, slabs], axis=0))
            part = jnp.sum(jnp.where(hi_row | lo_row, slabs.astype(F32), 0.0), axis=0, keepdims=True)
            total = part if g == 0 else total + part
        load.append(total)
        for s in range(segs):
            low = p * piece_w + s * seg_w
            out_ref[:, low : low + seg_w] = mixed[s * tok_rows : (s + 1) * tok_rows].astype(BF16)

    load_ref[...] = jnp.concatenate(load, axis=1)[:, :EXPERTS_ALL].reshape(EXPERTS_ALL)

    others(lambda d: token_copy(d, d).wait_send())
    for p in range(pieces):
        others(lambda d, p=p: back_copy(p, d, d).wait_send())


def copy_out(combined_in, load_in, combined_out, load_out):
    combined_out[...] = combined_in[...]
    load_out[...] = load_in[...]


def shards(tokens, expert_ids, gate_scores, gate_weight, up_weight, down_weight):
    n = lax.axis_size("exp")
    tok_rows, width = tokens.shape
    hid_dev = gate_weight.shape[1]
    spread = FF // hid_dev
    tiles = width // 128
    segs = max(s for s in range(1, SLAB // CAP + 1) if tiles % s == 0)
    pieces = 2 if tiles % (2 * segs) == 0 else 1
    piece_w = width // pieces
    seg_w = piece_w // segs
    groups = n // GROUP
    cfg = (n, spread, segs, pieces, piece_w, seg_w)
    dma = pltpu.SemaphoreType.DMA
    scratch = [
        pltpu.VMEM(tokens.shape, BF16),
        pltpu.VMEM(expert_ids.shape[::-1], jnp.int32),
        pltpu.VMEM(gate_scores.shape[::-1], F32),
        pltpu.VMEM((pieces, piece_w, hid_dev), BF16),
        pltpu.VMEM((pieces, piece_w, hid_dev), BF16),
        pltpu.VMEM((pieces, hid_dev, piece_w), BF16),
        pltpu.VMEM((n, SLAB, pieces * seg_w), BF16),
        pltpu.VMEM((n, SLAB, pieces * seg_w), BF16),
        pltpu.VMEM((pieces, n, SLAB, seg_w), BF16),
        pltpu.VMEM((pieces, n, SLAB, seg_w), BF16),
        pltpu.VMEM((SLAB // 2, pieces * seg_w), F32),
        pltpu.VMEM((groups, segs * tok_rows, 2 * GROUP * SLAB), BF16),
        pltpu.VMEM((n * CAP, piece_w), BF16),
        pltpu.VMEM((n * CAP, hid_dev), F32),
        pltpu.VMEM((n * CAP, hid_dev), F32),
        pltpu.VMEM((n * CAP, hid_dev), BF16),
        dma((3,)),
        dma((pieces,)),
        dma((pieces,)),
        dma((pieces,)),
        dma((n,)),
        dma((n,)),
        dma((pieces, n)),
        dma((pieces, n)),
    ]
    vmem = pl.BlockSpec(memory_space=pltpu.VMEM)
    out_shape = (
        jax.ShapeDtypeStruct(tokens.shape, BF16),
        jax.ShapeDtypeStruct((EXPERTS_ALL,), F32),
    )
    combined, load = pl.pallas_call(
        functools.partial(kernel, cfg),
        out_shape=out_shape,
        in_specs=[pl.BlockSpec(memory_space=pltpu.HBM)] * 6,
        out_specs=(vmem, vmem),
        scratch_shapes=scratch,
        compiler_params=pltpu.CompilerParams(
            collective_id=0, has_side_effects=True, vmem_limit_bytes=62 * 1024 * 1024
        ),
    )(tokens, expert_ids.T, gate_scores.T, gate_weight, up_weight, down_weight)
    return pl.pallas_call(
        copy_out,
        out_shape=out_shape,
        in_specs=[vmem, vmem],
        out_specs=(vmem, vmem),
    )(combined, load)


def solution(mesh):
    return jax.shard_map(
        shards,
        mesh=mesh,
        in_specs=(
            P(("rep", "exp"), None),
            P(("rep", "exp"), None),
            P(("rep", "exp"), None),
            P(None, "exp"),
            P(None, "exp"),
            P("exp", None),
        ),
        out_specs=(P(("rep", "exp"), None), P("rep")),
        check_vma=False,
    )
```

```python
import functools

import jax
import jax.numpy as jnp
from jax import lax
from jax.experimental import pallas as pl
from jax.experimental.pallas import tpu as pltpu
from jax.sharding import PartitionSpec as P

FF = 2048
EXPERTS_ALL = 384
CAP = 2
SLAB = 16
GROUP = 8
TILE = 256
MESH = pl.DeviceIdType.MESH
BF16 = jnp.bfloat16
F32 = jnp.float32


def dot(a, b):
    return jnp.dot(a, b, preferred_element_type=F32)


def iota(shape, dim):
    return lax.broadcasted_iota(jnp.int32, shape, dim)


def one_hot(mask):
    return jnp.where(mask, 1.0, 0.0).astype(BF16)


def slab_place(i, segs):
    dev, seg, row = i // SLAB, (i % SLAB) // CAP, i % CAP
    return jnp.where(seg < segs, seg * (GROUP * CAP) + dev * CAP + row, -1)


def kernel(
    cfg,
    tokens_hbm, ids_hbm, scores_hbm, gate_hbm, up_hbm, down_hbm,
    out_ref, load_ref,
    tokens_v, ids_v, scores_v, gate_v, up_v, down_v,
    send_v, arrived_v, back_v, returned_v, mass_v, mixing_v, x_v, gate_sum, up_sum, hidden_v, down_sum,
    small_sem, gate_sem, up_sem, down_sem,
    send_sem, recv_sem, back_send_sem, back_recv_sem,
):
    n, spread, segs, pieces, piece_w, seg_w, k_parts = cfg
    k_rows = down_hbm.shape[0] // k_parts
    groups = n // GROUP
    top, tok_rows = ids_v.shape
    me = lax.axis_index("exp")

    small = [
        pltpu.make_async_copy(ids_hbm, ids_v, small_sem.at[0]),
        pltpu.make_async_copy(scores_hbm, scores_v, small_sem.at[1]),
        pltpu.make_async_copy(tokens_hbm, tokens_v, small_sem.at[2]),
    ]
    for copy in small:
        copy.start()

    def gate_copy(p):
        return pltpu.make_async_copy(
            gate_hbm.at[pl.ds(p * piece_w, piece_w), :], gate_v.at[p], gate_sem.at[p]
        )

    def up_copy(p):
        return pltpu.make_async_copy(
            up_hbm.at[pl.ds(p * piece_w, piece_w), :], up_v.at[p], up_sem.at[p]
        )

    def down_copy(k):
        rows = pl.ds(k * k_rows, k_rows)
        return pltpu.make_async_copy(down_hbm.at[rows, :], down_v.at[rows, :], down_sem.at[k])

    gate_copy(0).start()
    up_copy(0).start()

    def others(body):
        def step(i, carry):
            body(lax.rem(me + i, n))
            return carry

        lax.fori_loop(1, n, step, 0, unroll=n <= 16)

    barrier = pltpu.get_barrier_semaphore()
    others(lambda d: pl.semaphore_signal(barrier, inc=1, device_id={"exp": d}, device_id_type=MESH))

    small[0].wait()
    slots = (n * CAP, tok_rows)
    slot_expert = iota(slots, 0) // (CAP * spread)
    hits = jnp.zeros(slots, F32)
    for k in range(top):
        hits = hits + jnp.where(ids_v[k : k + 1, :] == slot_expert, 1.0, 0.0)
    earlier = one_hot(iota((tok_rows, tok_rows), 0) < iota((tok_rows, tok_rows), 1))
    position = dot(hits.astype(BF16), earlier)
    placed = (hits > 0.5) & (position == (iota(slots, 0) % CAP).astype(F32))
    picker = one_hot(placed)

    slab_rows, packed_rows = GROUP * SLAB, segs * GROUP * CAP
    to_slab = one_hot(
        slab_place(iota((slab_rows, packed_rows), 0), segs) == iota((slab_rows, packed_rows), 1)
    )
    from_slab = one_hot(
        slab_place(iota((packed_rows, slab_rows), 1), segs) == iota((packed_rows, slab_rows), 0)
    )

    def pack(rows):
        packed = jnp.concatenate([rows[:, s * seg_w : (s + 1) * seg_w] for s in range(segs)], axis=0)
        return dot(to_slab, packed)

    small[2].wait()
    tokens = tokens_v[...]
    for g in range(groups):
        rows = picker[g * GROUP * CAP : (g + 1) * GROUP * CAP]
        picked = dot(rows, tokens).astype(BF16)
        for p in range(pieces):
            slabs = pack(picked[:, p * piece_w : (p + 1) * piece_w]).astype(BF16)
            send_v[g * GROUP : (g + 1) * GROUP, :, p * seg_w : (p + 1) * seg_w] = slabs.reshape(
                GROUP, SLAB, seg_w
            )

    def token_copy(d, src):
        return pltpu.make_async_remote_copy(
            src_ref=send_v.at[d], dst_ref=arrived_v.at[src],
            send_sem=send_sem.at[d], recv_sem=recv_sem.at[src],
            device_id={"exp": d}, device_id_type=MESH,
        )

    pl.semaphore_wait(barrier, n - 1)
    others(lambda d: token_copy(d, me).start())
    for p in range(1, pieces):
        gate_copy(p).start()
        up_copy(p).start()
    for k in range(k_parts):
        down_copy(k).start()
    arrived_v[me] = send_v[me]

    small[1].wait()
    ids = jnp.transpose(ids_v[...])
    scores = jnp.transpose(scores_v[...])
    mass_w = pieces * seg_w
    all_ids = iota((tok_rows, mass_w), 1)
    mass = jnp.zeros((tok_rows, mass_w), F32)
    for k in range(top):
        mass = mass + jnp.where(ids[:, k : k + 1] == all_ids, scores[:, k : k + 1], 0.0)
    mass = jnp.sum(mass, axis=0, keepdims=True)
    mass_hi = mass.astype(BF16).astype(F32)
    mass_v[0:1] = mass_hi
    mass_v[1:2] = mass - mass_hi
    slab_row = iota((slab_rows, seg_w), 0) % SLAB
    hi_row, lo_row = slab_row == SLAB - 2, slab_row == SLAB - 1

    gates = jnp.zeros(slots, F32)
    for k in range(top):
        found = ids_v[k : k + 1, :] == slot_expert
        gates = gates + jnp.where(found, scores_v[k : k + 1, :], 0.0)
    weights = jnp.where(placed, gates, 0.0)
    weights_hi = weights.astype(BF16)
    weights_lo = (weights - weights_hi.astype(F32)).astype(BF16)
    slab_lane = iota((n * CAP, slab_rows), 1)
    lane_seg = (iota((tok_rows, slab_rows), 1) % SLAB) // CAP
    for g in range(groups):
        slot_of = g * GROUP * CAP + slab_lane // SLAB * CAP + slab_lane % CAP
        spreading = one_hot(iota((n * CAP, slab_rows), 0) == slot_of)
        for part, term in enumerate((weights_hi, weights_lo)):
            wide = lax.dot_general(
                term, spreading, (((0,), (0,)), ((), ())), preferred_element_type=F32
            )
            for s in range(segs):
                mixing_v[
                    g, s * tok_rows : (s + 1) * tok_rows, part * slab_rows : (part + 1) * slab_rows
                ] = jnp.where(lane_seg == s, wide, 0.0).astype(BF16)

    hid_dev = hidden_v.shape[1]
    hid_tile = min(TILE, hid_dev)
    others(lambda d: token_copy(d, d).wait_recv())
    for p in range(pieces):
        for g in range(groups):
            slabs = arrived_v[g * GROUP : (g + 1) * GROUP, :, p * seg_w : (p + 1) * seg_w]
            packed = dot(from_slab, slabs.reshape(slab_rows, seg_w)).astype(BF16)
            size = GROUP * CAP
            for s in range(segs):
                x_v[g * size : (g + 1) * size, s * seg_w : (s + 1) * seg_w] = packed[
                    s * size : (s + 1) * size
                ]
        gate_copy(p).wait()
        up_copy(p).wait()

        def gate_up(j, carry, p=p):
            cols = pl.ds(pl.multiple_of(j * hid_tile, hid_tile), hid_tile)
            gate_act = dot(x_v[...], gate_v[p, :, cols])
            up_act = dot(x_v[...], up_v[p, :, cols])
            if p > 0:
                gate_act = gate_act + gate_sum[:, cols]
                up_act = up_act + up_sum[:, cols]
            if p < pieces - 1:
                gate_sum[:, cols] = gate_act
                up_sum[:, cols] = up_act
            else:
                silu = gate_act / (1.0 + jnp.exp(-gate_act))
                hidden_v[:, cols] = (silu * up_act).astype(BF16)
            return carry

        lax.fori_loop(0, hid_dev // hid_tile, gate_up, 0)

    def back_copy(p, d, src):
        return pltpu.make_async_remote_copy(
            src_ref=back_v.at[p, d], dst_ref=returned_v.at[p, src],
            send_sem=back_send_sem.at[p, d], recv_sem=back_recv_sem.at[p, src],
            device_id={"exp": d}, device_id_type=MESH,
        )

    def down(k, cols):
        at = slice(k * k_rows, (k + 1) * k_rows)
        return dot(hidden_v[:, at], down_v[at, cols])

    for k in range(k_parts - 1):
        down_copy(k).wait()
        for s in range(pieces * segs):
            cols = slice(s * seg_w, (s + 1) * seg_w)
            down_sum[:, cols] = down(k, cols) if k == 0 else down_sum[:, cols] + down(k, cols)
    down_copy(k_parts - 1).wait()
    for p in range(pieces):
        for s in range(segs):
            low = p * piece_w + s * seg_w
            cols = slice(low, low + seg_w)
            total = down(k_parts - 1, cols)
            if k_parts > 1:
                total = down_sum[:, cols] + total
            x_v[:, s * seg_w : (s + 1) * seg_w] = total.astype(BF16)
        for g in range(groups):
            rows = x_v[g * GROUP * CAP : (g + 1) * GROUP * CAP]
            at = slice(p * seg_w, (p + 1) * seg_w)
            spare = jnp.where(lo_row, mass_v[1:2, at], jnp.where(hi_row, mass_v[0:1, at], 0.0))
            slabs = (pack(rows) + spare).astype(BF16)
            back_v[p, g * GROUP : (g + 1) * GROUP] = slabs.reshape(GROUP, SLAB, seg_w)
        others(lambda d, p=p: back_copy(p, d, me).start())
        returned_v[p, me] = back_v[p, me]

    load = []
    for p in range(pieces):
        others(lambda d, p=p: back_copy(p, d, d).wait_recv())
        mixed = jnp.zeros((segs * tok_rows, seg_w), F32)
        for g in range(groups):
            slabs = returned_v[p, g * GROUP : (g + 1) * GROUP].reshape(slab_rows, seg_w)
            mixed = mixed + dot(mixing_v[g], jnp.concatenate([slabs, slabs], axis=0))
            part = jnp.sum(jnp.where(hi_row | lo_row, slabs.astype(F32), 0.0), axis=0, keepdims=True)
            total = part if g == 0 else total + part
        load.append(total)
        for s in range(segs):
            low = p * piece_w + s * seg_w
            out_ref[:, low : low + seg_w] = mixed[s * tok_rows : (s + 1) * tok_rows].astype(BF16)

    load_ref[...] = jnp.concatenate(load, axis=1)[:, :EXPERTS_ALL].reshape(EXPERTS_ALL)

    others(lambda d: token_copy(d, d).wait_send())
    for p in range(pieces):
        others(lambda d, p=p: back_copy(p, d, d).wait_send())


def copy_out(combined_in, load_in, combined_out, load_out):
    combined_out[...] = combined_in[...]
    load_out[...] = load_in[...]


def shards(tokens, expert_ids, gate_scores, gate_weight, up_weight, down_weight):
    n = lax.axis_size("exp")
    tok_rows, width = tokens.shape
    hid_dev = gate_weight.shape[1]
    spread = FF // hid_dev
    tiles = width // 128
    segs = max(s for s in range(1, SLAB // CAP + 1) if tiles % s == 0)
    pieces = 2 if tiles % (2 * segs) == 0 else 1
    piece_w = width // pieces
    seg_w = piece_w // segs
    groups = n // GROUP
    k_parts = 2 if hid_dev % 512 == 0 else 1
    cfg = (n, spread, segs, pieces, piece_w, seg_w, k_parts)
    dma = pltpu.SemaphoreType.DMA
    scratch = [
        pltpu.VMEM(tokens.shape, BF16),
        pltpu.VMEM(expert_ids.shape[::-1], jnp.int32),
        pltpu.VMEM(gate_scores.shape[::-1], F32),
        pltpu.VMEM((pieces, piece_w, hid_dev), BF16),
        pltpu.VMEM((pieces, piece_w, hid_dev), BF16),
        pltpu.VMEM((hid_dev, width), BF16),
        pltpu.VMEM((n, SLAB, pieces * seg_w), BF16),
        pltpu.VMEM((n, SLAB, pieces * seg_w), BF16),
        pltpu.VMEM((pieces, n, SLAB, seg_w), BF16),
        pltpu.VMEM((pieces, n, SLAB, seg_w), BF16),
        pltpu.VMEM((SLAB // 2, pieces * seg_w), F32),
        pltpu.VMEM((groups, segs * tok_rows, 2 * GROUP * SLAB), BF16),
        pltpu.VMEM((n * CAP, piece_w), BF16),
        pltpu.VMEM((n * CAP, hid_dev), F32),
        pltpu.VMEM((n * CAP, hid_dev), F32),
        pltpu.VMEM((n * CAP, hid_dev), BF16),
        pltpu.VMEM((n * CAP, width), F32),
        dma((3,)),
        dma((pieces,)),
        dma((pieces,)),
        dma((k_parts,)),
        dma((n,)),
        dma((n,)),
        dma((pieces, n)),
        dma((pieces, n)),
    ]
    vmem = pl.BlockSpec(memory_space=pltpu.VMEM)
    out_shape = (
        jax.ShapeDtypeStruct(tokens.shape, BF16),
        jax.ShapeDtypeStruct((EXPERTS_ALL,), F32),
    )
    combined, load = pl.pallas_call(
        functools.partial(kernel, cfg),
        out_shape=out_shape,
        in_specs=[pl.BlockSpec(memory_space=pltpu.HBM)] * 6,
        out_specs=(vmem, vmem),
        scratch_shapes=scratch,
        compiler_params=pltpu.CompilerParams(
            collective_id=0, has_side_effects=True, vmem_limit_bytes=62 * 1024 * 1024
        ),
    )(tokens, expert_ids.T, gate_scores.T, gate_weight, up_weight, down_weight)
    return pl.pallas_call(
        copy_out,
        out_shape=out_shape,
        in_specs=[vmem, vmem],
        out_specs=(vmem, vmem),
    )(combined, load)


def solution(mesh):
    return jax.shard_map(
        shards,
        mesh=mesh,
        in_specs=(
            P(("rep", "exp"), None),
            P(("rep", "exp"), None),
            P(("rep", "exp"), None),
            P(None, "exp"),
            P(None, "exp"),
            P("exp", None),
        ),
        out_specs=(P(("rep", "exp"), None), P("rep")),
        check_vma=False,
    )
```

```python
import functools

import jax
import jax.numpy as jnp
from jax import lax
from jax.experimental import pallas as pl
from jax.experimental.pallas import tpu as pltpu
from jax.sharding import PartitionSpec as P

FF = 2048
EXPERTS_ALL = 384
CAP = 2
SLAB = 16
GROUP = 8
TILE = 512
MESH = pl.DeviceIdType.MESH
BF16 = jnp.bfloat16
F32 = jnp.float32


def dot(a, b):
    return jnp.dot(a, b, preferred_element_type=F32)


def iota(shape, dim):
    return lax.broadcasted_iota(jnp.int32, shape, dim)


def one_hot(mask):
    return jnp.where(mask, 1.0, 0.0).astype(BF16)


def slab_place(i, segs):
    dev, seg, row = i // SLAB, (i % SLAB) // CAP, i % CAP
    return jnp.where(seg < segs, seg * (GROUP * CAP) + dev * CAP + row, -1)


def kernel(
    cfg,
    tokens_hbm, ids_hbm, scores_hbm, gate_hbm, up_hbm, down_hbm,
    out_ref, load_ref,
    tokens_v, ids_v, scores_v, gate_v, up_v, down_v,
    send_v, arrived_v, back_v, returned_v, mass_v, mixing_v, x_v, gate_sum, up_sum, hidden_v,
    small_sem, gate_sem, up_sem, down_sem,
    send_sem, recv_sem, back_send_sem, back_recv_sem,
):
    n, spread, segs, pieces, piece_w, seg_w = cfg
    groups = n // GROUP
    top, tok_rows = ids_v.shape
    me = lax.axis_index("exp")

    small = [
        pltpu.make_async_copy(ids_hbm, ids_v, small_sem.at[0]),
        pltpu.make_async_copy(scores_hbm, scores_v, small_sem.at[1]),
        pltpu.make_async_copy(tokens_hbm, tokens_v, small_sem.at[2]),
    ]
    for copy in small:
        copy.start()

    def gate_copy(p):
        return pltpu.make_async_copy(
            gate_hbm.at[pl.ds(p * piece_w, piece_w), :], gate_v.at[p], gate_sem.at[p]
        )

    def up_copy(p):
        return pltpu.make_async_copy(
            up_hbm.at[pl.ds(p * piece_w, piece_w), :], up_v.at[p], up_sem.at[p]
        )

    def down_copy(p):
        return pltpu.make_async_copy(
            down_hbm.at[:, pl.ds(p * piece_w, piece_w)], down_v.at[p], down_sem.at[p]
        )

    gate_copy(0).start()
    up_copy(0).start()

    def others(body):
        def step(i, carry):
            body(lax.rem(me + i, n))
            return carry

        lax.fori_loop(1, n, step, 0, unroll=n <= 16)

    barrier = pltpu.get_barrier_semaphore()
    others(lambda d: pl.semaphore_signal(barrier, inc=1, device_id={"exp": d}, device_id_type=MESH))

    small[0].wait()
    slots = (n * CAP, tok_rows)
    slot_expert = iota(slots, 0) // (CAP * spread)
    hits = jnp.zeros(slots, F32)
    for k in range(top):
        hits = hits + jnp.where(ids_v[k : k + 1, :] == slot_expert, 1.0, 0.0)
    earlier = one_hot(iota((tok_rows, tok_rows), 0) < iota((tok_rows, tok_rows), 1))
    position = dot(hits.astype(BF16), earlier)
    placed = (hits > 0.5) & (position == (iota(slots, 0) % CAP).astype(F32))
    picker = one_hot(placed)

    slab_rows, packed_rows = GROUP * SLAB, segs * GROUP * CAP
    to_slab = one_hot(
        slab_place(iota((slab_rows, packed_rows), 0), segs) == iota((slab_rows, packed_rows), 1)
    )
    from_slab = one_hot(
        slab_place(iota((packed_rows, slab_rows), 1), segs) == iota((packed_rows, slab_rows), 0)
    )

    def pack(rows):
        packed = jnp.concatenate([rows[:, s * seg_w : (s + 1) * seg_w] for s in range(segs)], axis=0)
        return dot(to_slab, packed)

    small[2].wait()
    tokens = tokens_v[...]
    for g in range(groups):
        rows = picker[g * GROUP * CAP : (g + 1) * GROUP * CAP]
        picked = dot(rows, tokens).astype(BF16)
        for p in range(pieces):
            slabs = pack(picked[:, p * piece_w : (p + 1) * piece_w]).astype(BF16)
            send_v[g * GROUP : (g + 1) * GROUP, :, p * seg_w : (p + 1) * seg_w] = slabs.reshape(
                GROUP, SLAB, seg_w
            )

    def token_copy(d, src):
        return pltpu.make_async_remote_copy(
            src_ref=send_v.at[d], dst_ref=arrived_v.at[src],
            send_sem=send_sem.at[d], recv_sem=recv_sem.at[src],
            device_id={"exp": d}, device_id_type=MESH,
        )

    pl.semaphore_wait(barrier, n - 1)
    others(lambda d: token_copy(d, me).start())
    for p in range(1, pieces):
        gate_copy(p).start()
        up_copy(p).start()
    for p in range(pieces):
        down_copy(p).start()
    arrived_v[me] = send_v[me]

    small[1].wait()
    ids = jnp.transpose(ids_v[...])
    scores = jnp.transpose(scores_v[...])
    mass_w = pieces * seg_w
    all_ids = iota((tok_rows, mass_w), 1)
    mass = jnp.zeros((tok_rows, mass_w), F32)
    for k in range(top):
        mass = mass + jnp.where(ids[:, k : k + 1] == all_ids, scores[:, k : k + 1], 0.0)
    mass = jnp.sum(mass, axis=0, keepdims=True)
    mass_hi = mass.astype(BF16).astype(F32)
    mass_v[0:1] = mass_hi
    mass_v[1:2] = mass - mass_hi
    slab_row = iota((slab_rows, seg_w), 0) % SLAB
    hi_row, lo_row = slab_row == SLAB - 2, slab_row == SLAB - 1

    gates = jnp.zeros(slots, F32)
    for k in range(top):
        found = ids_v[k : k + 1, :] == slot_expert
        gates = gates + jnp.where(found, scores_v[k : k + 1, :], 0.0)
    weights = jnp.where(placed, gates, 0.0)
    weights_hi = weights.astype(BF16)
    weights_lo = (weights - weights_hi.astype(F32)).astype(BF16)
    slab_lane = iota((n * CAP, slab_rows), 1)
    lane_seg = (iota((tok_rows, slab_rows), 1) % SLAB) // CAP
    for g in range(groups):
        slot_of = g * GROUP * CAP + slab_lane // SLAB * CAP + slab_lane % CAP
        spreading = one_hot(iota((n * CAP, slab_rows), 0) == slot_of)
        for part, term in enumerate((weights_hi, weights_lo)):
            wide = lax.dot_general(
                term, spreading, (((0,), (0,)), ((), ())), preferred_element_type=F32
            )
            for s in range(segs):
                mixing_v[
                    g, s * tok_rows : (s + 1) * tok_rows, part * slab_rows : (part + 1) * slab_rows
                ] = jnp.where(lane_seg == s, wide, 0.0).astype(BF16)

    hid_dev = hidden_v.shape[1]
    hid_tile = min(TILE, hid_dev)
    others(lambda d: token_copy(d, d).wait_recv())
    for p in range(pieces):
        for g in range(groups):
            slabs = arrived_v[g * GROUP : (g + 1) * GROUP, :, p * seg_w : (p + 1) * seg_w]
            packed = dot(from_slab, slabs.reshape(slab_rows, seg_w)).astype(BF16)
            size = GROUP * CAP
            for s in range(segs):
                x_v[g * size : (g + 1) * size, s * seg_w : (s + 1) * seg_w] = packed[
                    s * size : (s + 1) * size
                ]
        gate_copy(p).wait()
        up_copy(p).wait()

        def gate_up(j, carry, p=p):
            cols = pl.ds(pl.multiple_of(j * hid_tile, hid_tile), hid_tile)
            gate_act = dot(x_v[...], gate_v[p, :, cols])
            up_act = dot(x_v[...], up_v[p, :, cols])
            if p > 0:
                gate_act = gate_act + gate_sum[:, cols]
                up_act = up_act + up_sum[:, cols]
            if p < pieces - 1:
                gate_sum[:, cols] = gate_act
                up_sum[:, cols] = up_act
            else:
                silu = gate_act / (1.0 + jnp.exp(-gate_act))
                hidden_v[:, cols] = (silu * up_act).astype(BF16)
            return carry

        lax.fori_loop(0, hid_dev // hid_tile, gate_up, 0, unroll=2 if hid_dev > hid_tile else 1)

    def back_copy(p, d, src):
        return pltpu.make_async_remote_copy(
            src_ref=back_v.at[p, d], dst_ref=returned_v.at[p, src],
            send_sem=back_send_sem.at[p, d], recv_sem=back_recv_sem.at[p, src],
            device_id={"exp": d}, device_id_type=MESH,
        )

    for p in range(pieces):
        down_copy(p).wait()
        for s in range(segs):
            cols = slice(s * seg_w, (s + 1) * seg_w)
            x_v[:, cols] = dot(hidden_v[...], down_v[p, :, cols]).astype(BF16)
        for g in range(groups):
            rows = x_v[g * GROUP * CAP : (g + 1) * GROUP * CAP]
            at = slice(p * seg_w, (p + 1) * seg_w)
            spare = jnp.where(lo_row, mass_v[1:2, at], jnp.where(hi_row, mass_v[0:1, at], 0.0))
            slabs = (pack(rows) + spare).astype(BF16)
            back_v[p, g * GROUP : (g + 1) * GROUP] = slabs.reshape(GROUP, SLAB, seg_w)
        others(lambda d, p=p: back_copy(p, d, me).start())
        returned_v[p, me] = back_v[p, me]

    load = []
    for p in range(pieces):
        others(lambda d, p=p: back_copy(p, d, d).wait_recv())
        mixed = jnp.zeros((segs * tok_rows, seg_w), F32)
        for g in range(groups):
            slabs = returned_v[p, g * GROUP : (g + 1) * GROUP].reshape(slab_rows, seg_w)
            mixed = mixed + dot(mixing_v[g], jnp.concatenate([slabs, slabs], axis=0))
            part = jnp.sum(jnp.where(hi_row | lo_row, slabs.astype(F32), 0.0), axis=0, keepdims=True)
            total = part if g == 0 else total + part
        load.append(total)
        for s in range(segs):
            low = p * piece_w + s * seg_w
            out_ref[:, low : low + seg_w] = mixed[s * tok_rows : (s + 1) * tok_rows].astype(BF16)

    load_ref[...] = jnp.concatenate(load, axis=1)[:, :EXPERTS_ALL].reshape(EXPERTS_ALL)

    others(lambda d: token_copy(d, d).wait_send())
    for p in range(pieces):
        others(lambda d, p=p: back_copy(p, d, d).wait_send())


def copy_out(combined_in, load_in, combined_out, load_out):
    combined_out[...] = combined_in[...]
    load_out[...] = load_in[...]


def shards(tokens, expert_ids, gate_scores, gate_weight, up_weight, down_weight):
    n = lax.axis_size("exp")
    tok_rows, width = tokens.shape
    hid_dev = gate_weight.shape[1]
    spread = FF // hid_dev
    tiles = width // 128
    segs = max(s for s in range(1, SLAB // CAP + 1) if tiles % s == 0)
    pieces = 2 if tiles % (2 * segs) == 0 else 1
    piece_w = width // pieces
    seg_w = piece_w // segs
    groups = n // GROUP
    cfg = (n, spread, segs, pieces, piece_w, seg_w)
    dma = pltpu.SemaphoreType.DMA
    scratch = [
        pltpu.VMEM(tokens.shape, BF16),
        pltpu.VMEM(expert_ids.shape[::-1], jnp.int32),
        pltpu.VMEM(gate_scores.shape[::-1], F32),
        pltpu.VMEM((pieces, piece_w, hid_dev), BF16),
        pltpu.VMEM((pieces, piece_w, hid_dev), BF16),
        pltpu.VMEM((pieces, hid_dev, piece_w), BF16),
        pltpu.VMEM((n, SLAB, pieces * seg_w), BF16),
        pltpu.VMEM((n, SLAB, pieces * seg_w), BF16),
        pltpu.VMEM((pieces, n, SLAB, seg_w), BF16),
        pltpu.VMEM((pieces, n, SLAB, seg_w), BF16),
        pltpu.VMEM((SLAB // 2, pieces * seg_w), F32),
        pltpu.VMEM((groups, segs * tok_rows, 2 * GROUP * SLAB), BF16),
        pltpu.VMEM((n * CAP, piece_w), BF16),
        pltpu.VMEM((n * CAP, hid_dev), F32),
        pltpu.VMEM((n * CAP, hid_dev), F32),
        pltpu.VMEM((n * CAP, hid_dev), BF16),
        dma((3,)),
        dma((pieces,)),
        dma((pieces,)),
        dma((pieces,)),
        dma((n,)),
        dma((n,)),
        dma((pieces, n)),
        dma((pieces, n)),
    ]
    vmem = pl.BlockSpec(memory_space=pltpu.VMEM)
    out_shape = (
        jax.ShapeDtypeStruct(tokens.shape, BF16),
        jax.ShapeDtypeStruct((EXPERTS_ALL,), F32),
    )
    combined, load = pl.pallas_call(
        functools.partial(kernel, cfg),
        out_shape=out_shape,
        in_specs=[pl.BlockSpec(memory_space=pltpu.HBM)] * 6,
        out_specs=(vmem, vmem),
        scratch_shapes=scratch,
        compiler_params=pltpu.CompilerParams(
            collective_id=0, has_side_effects=True, vmem_limit_bytes=62 * 1024 * 1024
        ),
    )(tokens, expert_ids.T, gate_scores.T, gate_weight, up_weight, down_weight)
    return pl.pallas_call(
        copy_out,
        out_shape=out_shape,
        in_specs=[vmem, vmem],
        out_specs=(vmem, vmem),
    )(combined, load)


def solution(mesh):
    return jax.shard_map(
        shards,
        mesh=mesh,
        in_specs=(
            P(("rep", "exp"), None),
            P(("rep", "exp"), None),
            P(("rep", "exp"), None),
            P(None, "exp"),
            P(None, "exp"),
            P("exp", None),
        ),
        out_specs=(P(("rep", "exp"), None), P("rep")),
        check_vma=False,
    )
```
